128 devices in a mesh: batch: 4 (over y), seq: 8 (over z, core), tensor: 4 (over x).
Axes of the slice: x: 4, y: 4, z: 4, core: 2. Of those that a mesh axis runs over, the one named last changes fastest.
Arguments:
- inputs: float32 [8, 1024, 1024], P('batch', 'seq'), may hold values from -6 to 6
- decay_rate: float32 [8, 1024, 8], P('batch', 'seq', 'tensor'), may hold values from 0.1 to 1
- cotangent: bfloat16 [8, 1024, 1024], P('batch', 'seq'), may hold values from -6 to 6
- mix_gain: bfloat16 [1024], P(('batch', 'seq')), may hold values from 0.5 to 1.5
- query_weight: bfloat16 [1024, 1024], P(('batch', 'seq'), 'tensor'), may hold values from -0.1875 to 0.1875
- key_weight: bfloat16 [1024, 1024], P(('batch', 'seq'), 'tensor'), may hold values from -0.1875 to 0.1875
- value_weight: bfloat16 [1024, 2048], P(('batch', 'seq'), 'tensor'), may hold values from -0.1875 to 0.1875
- gate_weight: bfloat16 [1024, 2048], P(('batch', 'seq'), 'tensor'), may hold values from -0.1875 to 0.1875
- beta_weight: bfloat16 [1024, 8], P(('batch', 'seq'), 'tensor'), may hold values from -0.1875 to 0.1875
- conv_query: bfloat16 [1024, 4], P('tensor'), may hold values from -3 to 3
- conv_key: bfloat16 [1024, 4], P('tensor'), may hold values from -3 to 3
- conv_value: bfloat16 [2048, 4], P('tensor'), may hold values from -3 to 3
- out_gain: bfloat16 [2048], P('tensor'), may hold values from 0.5 to 1.5
- output_weight: bfloat16 [1024, 2048], P(('batch', 'seq'), 'tensor'), may hold values from -0.125 to 0.125
- ffn_gain: bfloat16 [1024], P(('batch', 'seq')), may hold values from 0.5 to 1.5
- ffn_gate: bfloat16 [1024, 2816], P(('batch', 'seq'), 'tensor'), may hold values from -0.1875 to 0.1875
- ffn_up: bfloat16 [1024, 2816], P(('batch', 'seq'), 'tensor'), may hold values from -0.1875 to 0.1875
- ffn_down: bfloat16 [1024, 2816], P(('batch', 'seq'), 'tensor'), may hold values from -0.109375 to 0.109375
Outputs:
- result: float32 [8, 1024, 1024], P('batch', 'seq')
- grad_inputs: float32 [8, 1024, 1024], P('batch', 'seq')
- grad_mix_gain: float32 [1024], P(('batch', 'seq'))
- grad_query_weight: float32 [1024, 1024], P(('batch', 'seq'), 'tensor')
- grad_key_weight: float32 [1024, 1024], P(('batch', 'seq'), 'tensor')
- grad_value_weight: float32 [1024, 2048], P(('batch', 'seq'), 'tensor')
- grad_gate_weight: float32 [1024, 2048], P(('batch', 'seq'), 'tensor')
- grad_beta_weight: float32 [1024, 8], P(('batch', 'seq'), 'tensor')
- grad_conv_query: float32 [1024, 4], P('tensor')
- grad_conv_key: float32 [1024, 4], P('tensor')
- grad_conv_value: float32 [2048, 4], P('tensor')
- grad_out_gain: float32 [2048], P('tensor')
- grad_output_weight: float32 [1024, 2048], P(('batch', 'seq'), 'tensor')
- grad_ffn_gain: float32 [1024], P(('batch', 'seq'))
- grad_ffn_gate: float32 [1024, 2816], P(('batch', 'seq'), 'tensor')
- grad_ffn_up: float32 [1024, 2816], P(('batch', 'seq'), 'tensor')
- grad_ffn_down: float32 [1024, 2816], P(('batch', 'seq'), 'tensor')
The draws below stay inside these ranges and needn't reach their ends.
All inputs are finite; a program needn't handle non-finite values.
Results may differ from the reference program's by a relative error of at most 0.025.
Values may be sent and summed in bfloat16 or wider, within the bound.
No kernel may reach another device: no remote copies, remote signals or barrier semaphores. Data moves between devices by JAX's collectives and lax.ppermute only.
A program may use at most 128 MiB of HBM per device.

```python
import jax
import jax.numpy as jnp
from jax import lax

D = 1024
H = 8
DK = 128
DV = 256
FF = 2816
KCONV = 4
BLOCK = 64
SEQ_LEN = 1024
NSEQ = 8


def draw_decay_rate(key, part):
    key = jax.random.fold_in(key, 7)
    span_key, rough_key, spot_key, level_key = jax.random.split(key, 4)
    lower, upper = (30.0, 4.0 * SEQ_LEN)
    spans = jnp.exp(jax.random.uniform(span_key, (NSEQ, 1, H), jnp.float32, jnp.log(lower), jnp.log(upper)))
    rough = jax.random.uniform(rough_key, (NSEQ, SEQ_LEN, H), jnp.float32, 0.5, 2.0)
    spots = jax.random.randint(spot_key, (NSEQ, 3, 1), 0, SEQ_LEN)
    levels = jax.random.uniform(level_key, (NSEQ, 3, 1), jnp.float32, 0.5, 0.8)
    places = jnp.arange(SEQ_LEN)[None, None, :]
    factor = jnp.prod(jnp.where(spots == places, levels, 1.0), axis=1)
    return (jnp.exp(-rough / spans) * factor[:, :, None]).astype(jnp.float32)


def block_scale(key, extent, cuts, smallest, top_value):
    loudness, own = 1.0, jax.random.fold_in(key, 6)
    for dim, parts in cuts:
        heights = jnp.exp(jax.random.uniform(jax.random.fold_in(own, dim), (parts,), jnp.float32, smallest / len(cuts), top_value / len(cuts)))
        loudness = loudness * jnp.repeat(heights, extent[dim] // parts).reshape([-1 if axis == dim else 1 for axis in range(len(extent))])
    return loudness


def gaussian(stream_key, shape, width, bound, cuts=(), dtype=jnp.bfloat16):
    entries = jax.random.normal(stream_key, shape, jnp.float32) * width
    if len(cuts) > 0:
        entries = block_scale(stream_key, shape, cuts, -0.22, 0.18) * entries
    return jnp.clip(entries, min=-bound, max=bound).astype(dtype)


def setup_inputs(seed: int = 0) -> dict:
    splits = jax.random.split(jax.random.key(seed), 19)
    inputs = gaussian(splits[0], (NSEQ, SEQ_LEN, D), 1.0, 6.0, ((0, 4), (1, 8)), jnp.float32)
    decay_rate = draw_decay_rate(jax.random.fold_in(splits[18], 71), 0)
    cotangent = gaussian(splits[2], (NSEQ, SEQ_LEN, D), 1.0, 6.0, ((0, 4), (1, 8)))
    mix_gain = jnp.clip(1.0 + 0.1 * jax.random.normal(splits[3], (D,), jnp.float32), 0.5, 1.5).astype(jnp.bfloat16)
    query_weight = gaussian(splits[4], (D, H * DK), D ** -0.5, 0.1875, ((0, 32), (1, 4)))
    key_weight = gaussian(splits[5], (D, H * DK), D ** -0.5, 0.1875, ((0, 32), (1, 4)))
    value_weight = gaussian(splits[6], (D, H * DV), D ** -0.5, 0.1875, ((0, 32), (1, 4)))
    gate_weight = gaussian(splits[7], (D, H * DV), D ** -0.5, 0.1875, ((0, 32), (1, 4)))
    beta_weight = gaussian(splits[8], (D, H), D ** -0.5, 0.1875, ((0, 32), (1, 4)))
    conv_query = gaussian(splits[9], (H * DK, KCONV), KCONV ** -0.5, 3.0, ((0, 4),))
    conv_key = gaussian(splits[10], (H * DK, KCONV), KCONV ** -0.5, 3.0, ((0, 4),))
    conv_value = gaussian(splits[11], (H * DV, KCONV), KCONV ** -0.5, 3.0, ((0, 4),))
    out_gain = jnp.clip(1.0 + 0.1 * jax.random.normal(splits[12], (H * DV,), jnp.float32), 0.5, 1.5).astype(jnp.bfloat16)
    output_weight = gaussian(splits[13], (D, H * DV), (H * DV) ** -0.5, 0.125, ((0, 32), (1, 4)))
    ffn_gain = jnp.clip(1.0 + 0.1 * jax.random.normal(splits[14], (D,), jnp.float32), 0.5, 1.5).astype(jnp.bfloat16)
    ffn_gate = gaussian(splits[15], (D, FF), D ** -0.5, 0.1875, ((0, 32), (1, 4)))
    ffn_up = gaussian(splits[16], (D, FF), D ** -0.5, 0.1875, ((0, 32), (1, 4)))
    ffn_down = gaussian(splits[17], (D, FF), FF ** -0.5, 0.109375, ((0, 32), (1, 4)))
    return {"inputs": inputs, "decay_rate": decay_rate, "cotangent": cotangent, "mix_gain": mix_gain, "query_weight": query_weight, "key_weight": key_weight, "value_weight": value_weight, "gate_weight": gate_weight, "beta_weight": beta_weight, "conv_query": conv_query, "conv_key": conv_key, "conv_value": conv_value, "out_gain": out_gain, "output_weight": output_weight, "ffn_gain": ffn_gain, "ffn_gate": ffn_gate, "ffn_up": ffn_up, "ffn_down": ffn_down}


epsilon = 1e-06
highest_precision = lax.Precision.HIGHEST

@jax.custom_vjp
def low(v):
    return lax.optimization_barrier(v.astype(jnp.bfloat16)).astype(jnp.float32)

@jax.custom_vjp
def low_back(v):
    return v

def low_keep(v):
    return (low(v), None)

def low_pass(kept, grad):
    return (grad,)

def back_keep(v):
    return (v, None)

def back_low(kept, grad):
    return (low(grad),)
low.defvjp(low_keep, low_pass)
low_back.defvjp(back_keep, back_low)

def dense(first_op, second_op):
    return jnp.dot(first_op, second_op, precision=highest_precision, preferred_element_type=jnp.float32)

def rms_scale(values, gain_vector):
    return values * lax.rsqrt(lax.optimization_barrier(jnp.mean(values * values, -1, keepdims=True)) + epsilon) * gain_vector

def causal(projected, kernel):
    padded = jnp.pad(projected, ((KCONV - 1, 0), (0, 0)))
    length = projected.shape[0]
    summed = jnp.zeros_like(projected)
    for offset in range(KCONV):
        summed = summed + padded[offset:offset + length] * kernel[:, offset]
    return jax.nn.silu(summed)

def unit_rows(values):
    return values * lax.rsqrt(lax.optimization_barrier(jnp.sum(values * values, -1, keepdims=True)) + epsilon)

def delta_rule(queries, key_rows, value_rows, beta_gate, decay_rate):
    query_factor = DK ** (-0.5)
    block_count = queries.shape[0] // BLOCK

    def split_blocks(values):
        return values.reshape((block_count, BLOCK) + values.shape[1:])

    def one_token(memory_state, inputs):
        query_current, key_current, value_t, beta_t, decay_t = inputs
        key_lookup = jnp.einsum('uy,uyl->ul', key_current, memory_state, precision=highest_precision)
        memory_state = decay_t[:, None, None] * (memory_state - beta_t[:, None, None] * key_current[:, :, None] * key_lookup[:, None, :]) + beta_t[:, None, None] * key_current[:, :, None] * value_t[:, None, :]
        return (memory_state, query_factor * jnp.einsum('uy,uyl->ul', query_current, memory_state, precision=highest_precision))

    def one_block(memory_state, inputs):
        return lax.scan(one_token, memory_state, inputs)
    zero_state = jnp.zeros((queries.shape[1], DK, DV), jnp.float32)
    pieces = tuple((split_blocks(item) for item in (queries, key_rows, value_rows, beta_gate, decay_rate)))
    final_state, mixed = lax.scan(jax.checkpoint(one_block), zero_state, pieces)
    return mixed.reshape((block_count * BLOCK,) + mixed.shape[2:])

def layer(inputs, decay_rate, weights):
    mix_gain, query_weight, key_weight, value_weight, gate_weight, beta_weight, conv_query, conv_key, conv_value, out_gain, output_weight, ffn_gain, ffn_gate, ffn_up, ffn_down = weights
    length = inputs.shape[0]
    mix_input = low(rms_scale(inputs, mix_gain))
    proj_query = low_back(low(dense(mix_input, query_weight)))
    proj_key = low_back(low(dense(mix_input, key_weight)))
    proj_value = low_back(low(dense(mix_input, value_weight)))
    gate_logit = low_back(dense(mix_input, gate_weight))
    beta_logit = low_back(dense(mix_input, beta_weight))
    queries = low(unit_rows(causal(proj_query, conv_query).reshape(length, H, DK)))
    key_rows = low(unit_rows(causal(proj_key, conv_key).reshape(length, H, DK)))
    value_rows = low(causal(proj_value, conv_value).reshape(length, H, DV))
    mixed = delta_rule(queries, key_rows, value_rows, jax.nn.sigmoid(beta_logit), decay_rate)
    normed = mixed * lax.rsqrt(lax.optimization_barrier(jnp.mean(mixed * mixed, -1, keepdims=True)) + epsilon)
    gated = low(normed.reshape(length, H * DV) * out_gain * jax.nn.silu(gate_logit))
    middle = inputs + low_back(dense(gated, output_weight.T))
    ffn_input = low(rms_scale(middle, ffn_gain))
    gate_act = low_back(dense(ffn_input, ffn_gate))
    up_act = low_back(dense(ffn_input, ffn_up))
    hidden = low(jax.nn.silu(gate_act) * up_act)
    return middle + low_back(dense(hidden, ffn_down.T))

def reference(inputs, decay_rate, cotangent, mix_gain, query_weight, key_weight, value_weight, gate_weight, beta_weight, conv_query, conv_key, conv_value, out_gain, output_weight, ffn_gain, ffn_gate, ffn_up, ffn_down):
    weights = tuple((item.astype(jnp.float32) for item in (mix_gain, query_weight, key_weight, value_weight, gate_weight, beta_weight, conv_query, conv_key, conv_value, out_gain, output_weight, ffn_gain, ffn_gate, ffn_up, ffn_down)))

    def one_sequence(totals, item):
        seq_inputs, seq_decay, seq_cotangent = item
        outcome, pull = jax.vjp(lambda values, params: layer(values, seq_decay, params), seq_inputs, weights)
        grad_values, grad_params = pull(seq_cotangent.astype(jnp.float32))
        totals = tuple((first + second for first, second in zip(totals, grad_params)))
        return (totals, (outcome, grad_values))
    zero_totals = tuple((jnp.zeros_like(item) for item in weights))
    totals, (result, grad_inputs) = lax.scan(one_sequence, zero_totals, (inputs, decay_rate, cotangent))
    return (result, grad_inputs, totals[0], totals[1], totals[2], totals[3], totals[4], totals[5], totals[6], totals[7], totals[8], totals[9], totals[10], totals[11], totals[12], totals[13], totals[14])
```

```python
import jax
import jax.numpy as jnp
from jax import lax
from jax.experimental import pallas as pl
from jax.experimental.pallas import tpu as pltpu
from jax.sharding import PartitionSpec as P

bf16 = jnp.bfloat16
f32 = jnp.float32

DK = 128
DV = 256
HV = 128
KCONV = 4
CHUNK = 128
NCHUNK = 8
CHUNK_ROWS = CHUNK + 16
CHAN = 2 * DK + HV
W1_COLS = 1664
W2_COLS = 2816
FFP = 768
EPS = 1e-06
QF = DK ** (-0.5)
VMEM_LIMIT = 56 * 1024 * 1024


def move_core(v):
    return lax.ppermute(v, "seq", [(i, i ^ 1) for i in range(8)])


def move_z(v, d):
    return lax.ppermute(v, "seq", [(i, (i + 2 * d) % 8) for i in range(8)])


def move_y(v, d):
    return lax.ppermute(v, "batch", [(i, (i + d) % 4) for i in range(4)])


def move_x(v, d):
    return lax.ppermute(v, "tensor", [(i, (i + d) % 4) for i in range(4)])


def swap_z(v, m):
    return lax.ppermute(v, "seq", [(i, i ^ (2 * m)) for i in range(8)])


def swap_y(v, m):
    return lax.ppermute(v, "batch", [(i, i ^ m) for i in range(4)])


def swap_x(v, m):
    return lax.ppermute(v, "tensor", [(i, i ^ m) for i in range(4)])


def sum4(v, swap):
    return (v + swap(v, 1)) + (swap(v, 2) + swap(v, 3))


def pick(v, i):
    return lax.dynamic_index_in_dim(v, i, 0, keepdims=False)


def scatter_x(partial, x):
    got = [move_x(pick(partial, (x + d) % 4), d) for d in (1, 2, 3)]
    own = pick(partial, x).astype(f32)
    return own + got[0].astype(f32) + got[1].astype(f32) + got[2].astype(f32)


def gather_x(rows):
    return [rows] + [move_x(rows, d) for d in (1, 2, 3)]


def in_order(blocks, x):
    out = jnp.zeros((4,) + blocks[0].shape, blocks[0].dtype)
    for d in range(4):
        out = lax.dynamic_update_index_in_dim(out, blocks[d], (x - d) % 4, 0)
    return out


def scatter_rows(mine, other, y, z):
    total = (mine.astype(f32) + move_core(other).astype(f32)).astype(bf16)
    a, b = total[:, :, 0], total[:, :, 1].swapaxes(0, 1)
    ra = pick(a, y).astype(f32)
    rb = pick(b, z).astype(f32)
    for d in (1, 2, 3):
        ra = ra + move_y(pick(a, (y + d) % 4), d).astype(f32)
        rb = rb + move_z(pick(b, (z + d) % 4), d).astype(f32)
    ra, rb = ra.astype(bf16), rb.astype(bf16)
    oa = pick(ra, z).astype(f32)
    ob = pick(rb, y).astype(f32)
    for d in (1, 2, 3):
        oa = oa + move_z(pick(ra, (z + d) % 4), d).astype(f32)
        ob = ob + move_y(pick(rb, (y + d) % 4), d).astype(f32)
    return jnp.concatenate([oa, ob], 0)


def mm(a, b):
    return jnp.dot(a.astype(bf16), b.astype(bf16), preferred_element_type=f32)


def mm_nt(a, b):
    return lax.dot_general(
        a.astype(bf16), b.astype(bf16), (((1,), (1,)), ((), ())), preferred_element_type=f32
    )


def mm_tn(a, b):
    return lax.dot_general(
        a.astype(bf16), b.astype(bf16), (((0,), (0,)), ((), ())), preferred_element_type=f32
    )


def halves(v):
    hi = v.astype(bf16)
    return hi, (v - hi.astype(f32)).astype(bf16)


def mm3(a, b):
    (ah, al), (bh, bl) = a, b
    return mm(ah, bh) + (mm(ah, bl) + mm(al, bh))


def sigmoid(v):
    return 1.0 / (1.0 + jnp.exp(-v))


def project_kernel(*refs):
    own_a, own_b, sib_a, sib_b = refs[0:4], refs[4:8], refs[8:12], refs[12:16]
    x_ref = refs[16]
    w_ref, mix_ref, send_ref, gate_ref, gain_ref, sem = refs[17:]
    y = lax.axis_index("batch")
    s = lax.axis_index("seq")
    z, core = s // 2, s % 2
    copies = []
    for far in range(4):
        for near in range(4):
            ya, za = (y - near + 4) % 4, (z - far + 4) % 4
            yb, zb = (y - far + 4) % 4, (z - near + 4) % 4
            for group, c in ((0, core), (1, 1 - core)):
                src_a = (own_a, sib_a)[group][far]
                src_b = (own_b, sib_b)[group][far]
                row_a = pl.multiple_of(ya * 256 + za * 64 + c * 32, 16)
                row_b = pl.multiple_of(yb * 256 + zb * 64 + c * 32 + 16, 16)
                copies.append(
                    pltpu.make_async_copy(src_a.at[near], w_ref.at[pl.ds(row_a, 16)], sem.at[len(copies)])
                )
                copies.append(
                    pltpu.make_async_copy(src_b.at[near], w_ref.at[pl.ds(row_b, 16)], sem.at[len(copies)])
                )
    for copy in copies:
        copy.start()
    xs = x_ref[...]
    normed = xs * lax.rsqrt(jnp.mean(xs * xs, -1, keepdims=True) + EPS)
    for copy in copies:
        copy.wait()
    last = w_ref[:, 1536:1664]
    row = lax.broadcasted_iota(jnp.int32, (8, 128), 0)
    lane = lax.broadcasted_iota(jnp.int32, (8, 128), 1)
    chosen = jnp.where(lane == row + 2, 1.0, 0.0).astype(bf16)
    gains = mm_nt(chosen, last)
    gain_ref[...] = gains
    mix = (normed * gains[0:1]).astype(bf16)
    mix_ref[...] = mix
    for first, head in ((0, 0), (128, 1)):
        q = jnp.dot(mix, w_ref[:, first : first + 128], preferred_element_type=f32).astype(bf16)
        k = jnp.dot(mix, w_ref[:, 256 + first : 384 + first], preferred_element_type=f32).astype(bf16)
        v = jnp.dot(
            mix, w_ref[:, 512 + head * 256 : 768 + head * 256], preferred_element_type=f32
        ).astype(bf16)
        for seq in range(2):
            for u in range(2):
                j = 4 * seq + 2 * head + u
                rows = slice(seq * CHUNK, (seq + 1) * CHUNK)
                send_ref[j, 0:CHUNK, 0:128] = q[rows]
                send_ref[j, 0:CHUNK, 128:256] = k[rows]
                send_ref[j, 0:CHUNK, 256:384] = v[rows, u * 128 : (u + 1) * 128]
    logit = lax.dot_general(
        last, mix, (((0,), (1,)), ((), ())), preferred_element_type=f32
    )
    row16 = lax.broadcasted_iota(jnp.int32, (16, 128), 0)
    for j in range(8):
        seq, head = j // 4, (j // 2) % 2
        b = logit[head : head + 1, seq * CHUNK : (seq + 1) * CHUNK]
        hi = b.astype(bf16).astype(f32)
        tile = jnp.where(row16 == 0, hi, jnp.where(row16 == 1, b - hi, 0.0))
        send_ref[j, CHUNK:CHUNK_ROWS, 0:128] = tile.astype(bf16)
        send_ref[j, CHUNK:CHUNK_ROWS, 128:384] = jnp.zeros((16, 256), bf16)
    gate_ref[...] = jnp.dot(mix, w_ref[:, 1024:1536], preferred_element_type=f32)


def masks():
    i = lax.broadcasted_iota(jnp.int32, (CHUNK, CHUNK), 0)
    j = lax.broadcasted_iota(jnp.int32, (CHUNK, CHUNK), 1)
    return i, j


def inverses(systems, i, j):
    split = [halves(n) for n in systems]
    pair = (i >> 1) == (j >> 1)
    unit = jnp.where(i == j, 1.0, 0.0)
    out = [unit - jnp.where(pair, n, 0.0) for n in systems]
    for level in range(1, 7):
        corner = ((i >> (level + 1)) == (j >> (level + 1))) & ((i >> level) != (j >> level))
        zero = jnp.zeros((CHUNK, CHUNK), bf16)
        for c in range(len(systems)):
            below = tuple(jnp.where(corner, part, zero) for part in split[c])
            now = halves(out[c])
            out[c] = out[c] - mm3(halves(mm3(now, below)), now)
    return out


def beta_columns(recv_ref):
    rows = [
        recv_ref[c, CHUNK : CHUNK + 16, 0:128].astype(f32)[0:2].sum(0, keepdims=True)
        for c in range(NCHUNK)
    ]
    return sigmoid(jnp.concatenate(rows, 0).T)


def load_tokens(recv_ref, ext):
    ext[0:16, :] = jnp.zeros((16, CHAN), f32)
    for c in range(NCHUNK):
        ext[16 + c * CHUNK : 16 + (c + 1) * CHUNK, :] = recv_ref[c, 0:CHUNK, :].astype(f32)


def convolve(ext, taps, c):
    first = 16 + c * CHUNK - (KCONV - 1)
    pre = ext[pl.ds(first, CHUNK), :] * taps[0:1]
    for tap in range(1, KCONV):
        pre = pre + ext[pl.ds(first + tap, CHUNK), :] * taps[tap : tap + 1]
    return pre


def unit(a):
    scale = lax.rsqrt(jnp.sum(a * a, -1, keepdims=True) + EPS)
    return a * scale, scale


def spread_of(lrows, lcols, c, i, j):
    gap = lcols[:, c : c + 1] - lrows[c : c + 1, :]
    return jnp.where(i >= j, jnp.exp(jnp.where(i >= j, gap, 0.0)), 0.0)


def forward_kernel(recv_ref, taps_ref, l_ref, mixed_ref, inv_ref, w_ref, u_ref, s_ref, ext):
    load_tokens(recv_ref, ext)
    taps = taps_ref[...]
    lrows = l_ref[...]
    lcols = lrows.T
    betas = beta_columns(recv_ref)
    i, j = masks()
    strict = i > j
    qs, ks, kds, ps, systems, rights, grown = [], [], [], [], [], [], []
    for c in range(NCHUNK):
        pre = convolve(ext, taps, c)
        act = pre * sigmoid(pre)
        q = unit(act[:, 0:128])[0].astype(bf16)
        k = unit(act[:, 128:256])[0].astype(bf16)
        v = act[:, 256:384].astype(bf16)
        spread = spread_of(lrows, lcols, c, i, j)
        beta = betas[:, c : c + 1]
        lcol = lcols[:, c : c + 1]
        ltop = lrows[c : c + 1, CHUNK - 1 : CHUNK]
        grow = jnp.exp(lcol)
        kf = k.astype(f32)
        systems.append(jnp.where(strict, beta * spread * mm_nt(k, k), 0.0))
        ps.append((spread * mm_nt(q, k)).astype(bf16))
        rights.append(
            jnp.concatenate([beta * v.astype(f32), (beta * grow) * kf], 1).astype(bf16)
        )
        qs.append((grow * q.astype(f32)).astype(bf16))
        kds.append((jnp.exp(ltop - lcol) * kf).astype(bf16))
        grown.append(jnp.exp(ltop))
    inv = inverses(systems, i, j)
    us, ws = [], []
    for c in range(NCHUNK):
        low = inv[c].astype(bf16)
        inv_ref[c] = low
        both = mm(low, rights[c])
        us.append(both[:, 0:128])
        ws.append(both[:, 128:256].astype(bf16))
        w_ref[c] = ws[c]
    state = jnp.zeros((DK, HV), f32)
    for c in range(NCHUNK):
        start = state.astype(bf16)
        s_ref[c] = start
        u = (us[c] - mm(ws[c], start)).astype(bf16)
        u_ref[c] = u
        state = grown[c] * state + mm_tn(kds[c], u)
        mixed_ref[c] = (QF * (mm(qs[c], start) + mm(ps[c], u))).astype(bf16)


def backward_kernel(
    recv_ref, taps_ref, l_ref, grad_ref, inv_ref, w_ref, u_ref, s_ref, out_ref, tap_ref, ext, gext
):
    load_tokens(recv_ref, ext)
    taps = taps_ref[...]
    lrows = l_ref[...]
    lcols = lrows.T
    betas = beta_columns(recv_ref)
    i, j = masks()
    strict = i > j
    gext[16 + NCHUNK * CHUNK :, :] = jnp.zeros((16, CHAN), f32)
    kept = []
    for c in range(NCHUNK):
        pre = convolve(ext, taps, c)
        sig = sigmoid(pre)
        act = pre * sig
        q = unit(act[:, 0:128])[0].astype(bf16)
        k = unit(act[:, 128:256])[0].astype(bf16)
        spread = spread_of(lrows, lcols, c, i, j)
        lcol = lcols[:, c : c + 1]
        ltop = lrows[c : c + 1, CHUNK - 1 : CHUNK]
        grow = jnp.exp(lcol)
        fade = jnp.exp(ltop - lcol)
        p = (spread * mm_nt(q, k)).astype(bf16)
        kd = (fade * k.astype(f32)).astype(bf16)
        grown_q = (QF * grow * q.astype(f32)).astype(bf16)
        g = grad_ref[c]
        du = QF * mm_tn(p, g)
        ds = mm_tn(grown_q, g)
        kept.append((q, k, grow, fade, jnp.exp(ltop), kd, du, ds))
    state = jnp.zeros((DK, HV), f32)
    after, dus = [None] * NCHUNK, [None] * NCHUNK
    for c in reversed(range(NCHUNK)):
        top, kd, du, ds = kept[c][4:]
        low = state.astype(bf16)
        after[c] = low
        du = (du + mm(kd, low)).astype(bf16)
        dus[c] = du
        state = top * state + ds - mm_tn(w_ref[c], du)
    cols = []
    for c in range(NCHUNK):
        q, k, grow, fade = kept[c][:4]
        beta = betas[:, c : c + 1]
        spread = spread_of(lrows, lcols, c, i, j)
        g = grad_ref[c]
        u = u_ref[c]
        start = s_ref[c]
        pre = convolve(ext, taps, c)
        sig = sigmoid(pre)
        act = pre * sig
        v = act[:, 256:384].astype(bf16).astype(f32)
        dr = mm_tn(inv_ref[c], dus[c])
        drl = dr.astype(bf16)
        dp = (QF * spread * mm_nt(g, u)).astype(bf16)
        dt = jnp.where(strict, -spread * mm_nt(drl, u), 0.0)
        dkk = (beta * dt).astype(bf16)
        recalled = grow * mm(k, start)
        cols.append(
            jnp.sum(dt * mm_nt(k, k), -1, keepdims=True)
            + jnp.sum(dr * (v - recalled), -1, keepdims=True)
        )
        dq = mm(dp, k) + (QF * grow) * mm_nt(g, start)
        dk = (
            mm_tn(dp, q)
            + fade * mm_nt(u, after[c])
            + (mm(dkk, k) + mm_tn(dkk, k))
            - (beta * grow) * mm_nt(drl, start)
        )
        dv = beta * dr
        slope = sig * (1.0 + pre * (1.0 - sig))
        for first, part in ((0, dq), (128, dk)):
            a = act[:, first : first + 128]
            n, scale = unit(a)
            da = scale * (part - n * jnp.sum(n * part, -1, keepdims=True))
            gext[16 + c * CHUNK : 16 + (c + 1) * CHUNK, first : first + 128] = (
                da * slope[:, first : first + 128]
            )
        gext[16 + c * CHUNK : 16 + (c + 1) * CHUNK, 256:384] = dv * slope[:, 256:384]
    dbeta = jnp.concatenate(cols, 1) * betas * (1.0 - betas)
    brows = dbeta.T
    row16 = lax.broadcasted_iota(jnp.int32, (16, 128), 0)
    tap_sums = [jnp.zeros((1, CHAN), f32) for _ in range(KCONV)]
    for c in range(NCHUNK):
        here = 16 + c * CHUNK
        gpre = gext[here : here + CHUNK, :]
        total = gpre * taps[KCONV - 1 : KCONV]
        tap_sums[KCONV - 1] = tap_sums[KCONV - 1] + jnp.sum(
            gpre * ext[here : here + CHUNK, :], 0, keepdims=True
        )
        for tap in range(KCONV - 1):
            back = KCONV - 1 - tap
            total = total + gext[pl.ds(here + back, CHUNK), :] * taps[tap : tap + 1]
            tap_sums[tap] = tap_sums[tap] + jnp.sum(
                gpre * ext[pl.ds(here - back, CHUNK), :], 0, keepdims=True
            )
        out_ref[c, 0:CHUNK, :] = total.astype(bf16)
        b = brows[c : c + 1, :]
        hi = b.astype(bf16).astype(f32)
        tile = jnp.where(row16 == 0, hi, jnp.where(row16 == 1, b - hi, 0.0))
        out_ref[c, CHUNK:CHUNK_ROWS, 0:128] = tile.astype(bf16)
        out_ref[c, CHUNK:CHUNK_ROWS, 128:384] = jnp.zeros((16, 256), bf16)
    tap_ref[...] = jnp.concatenate(tap_sums + [jnp.zeros((8 - KCONV, CHAN), f32)], 0)


def head_parts(mixed_ref, gate_ref, gain, seq, head):
    a = mixed_ref[4 * seq + 2 * head].astype(f32)
    b = mixed_ref[4 * seq + 2 * head + 1].astype(f32)
    mean = (jnp.sum(a * a, -1, keepdims=True) + jnp.sum(b * b, -1, keepdims=True)) / DV
    scale = lax.rsqrt(mean + EPS)
    logit = gate_ref[seq * CHUNK : (seq + 1) * CHUNK, head * DV : (head + 1) * DV]
    n = jnp.concatenate([a, b], 1) * scale
    return n, scale, logit, sigmoid(logit), gain[:, head * DV : (head + 1) * DV]


def output_kernel(mixed_ref, gate_ref, gain_ref, w_ref, gated_ref, part_ref):
    gain = gain_ref[0:1, :]
    for seq in range(2):
        for head in range(2):
            n, _, logit, sig, own = head_parts(mixed_ref, gate_ref, gain, seq, head)
            gated_ref[seq * CHUNK : (seq + 1) * CHUNK, head * DV : (head + 1) * DV] = (
                n * own * (logit * sig)
            ).astype(bf16)
    part_ref[...] = mm_nt(gated_ref[...], w_ref[...]).astype(bf16)


def output_back_kernel(
    gmix_ref, mixed_ref, gate_ref, gain_ref, w_ref, gmixed_ref, glogit_ref, ggain_ref
):
    gain = gain_ref[0:1, :]
    grad = jnp.dot(gmix_ref[...], w_ref[...], preferred_element_type=f32)
    sums = []
    for head in range(2):
        total = jnp.zeros((1, DV), f32)
        for seq in range(2):
            n, scale, logit, sig, own = head_parts(mixed_ref, gate_ref, gain, seq, head)
            g = grad[seq * CHUNK : (seq + 1) * CHUNK, head * DV : (head + 1) * DV]
            t = g * (logit * sig)
            total = total + jnp.sum(t * n, 0, keepdims=True)
            gn = t * own
            gm = scale * (gn - n * jnp.mean(gn * n, -1, keepdims=True))
            gmixed_ref[4 * seq + 2 * head] = gm[:, 0:128].astype(bf16)
            gmixed_ref[4 * seq + 2 * head + 1] = gm[:, 128:256].astype(bf16)
            slope = sig * (1.0 + logit * (1.0 - sig))
            glogit_ref[seq * CHUNK : (seq + 1) * CHUNK, head * DV : (head + 1) * DV] = (
                g * n * own * slope
            ).astype(bf16)
        sums.append(total)
    ggain_ref[...] = jnp.broadcast_to(jnp.concatenate(sums, 1), (8, 2 * DV))


def ffn_kernel(in_ref, cot_ref, w_ref, part_ref, gpart_ref, hidden_ref, ggate_ref, gup_ref):
    tokens = in_ref[...]
    gate = jnp.dot(tokens, w_ref[:, 512 : 512 + FFP], preferred_element_type=f32)
    up = jnp.dot(tokens, w_ref[:, 512 + FFP : 512 + 2 * FFP], preferred_element_type=f32)
    down = w_ref[:, 512 + 2 * FFP :]
    ghidden = jnp.dot(cot_ref[...], down, preferred_element_type=f32)
    sig = sigmoid(gate)
    silu = gate * sig
    ggate = (ghidden * up * (sig * (1.0 + gate * (1.0 - sig)))).astype(bf16)
    gup = (ghidden * silu).astype(bf16)
    hidden = (silu * up).astype(bf16)
    hidden_ref[...] = hidden
    ggate_ref[...] = ggate
    gup_ref[...] = gup
    gpart_ref[...] = (
        mm_nt(ggate, w_ref[:, 512 : 512 + FFP]) + mm_nt(gup, w_ref[:, 512 + FFP : 512 + 2 * FFP])
    ).astype(bf16)
    part_ref[...] = mm_nt(hidden, down).astype(bf16)


def core_split(value, core):
    cols = value.shape[-1]
    value = value.reshape(4, 2, 2, 16, cols)
    first, second = value[:, 0], value[:, 1]
    return jnp.where(core == 0, first, second), jnp.where(core == 0, second, first)


def project_back_kernel(recv_ref, glogit_ref, mix_ref, dproj_ref, mine_ref, other_ref):
    core = lax.axis_index("seq") % 2
    row = lax.broadcasted_iota(jnp.int32, (128, 128), 0)
    for seq in range(2):
        rows = slice(seq * CHUNK, (seq + 1) * CHUNK)
        beta = jnp.zeros((128, 128), f32)
        for head in range(2):
            ja = 4 * seq + 2 * head
            a = recv_ref[ja].astype(f32)
            b = recv_ref[ja + 1].astype(f32)
            dproj_ref[rows, head * 128 : (head + 1) * 128] = (
                a[0:CHUNK, 0:128] + b[0:CHUNK, 0:128]
            ).astype(bf16)
            dproj_ref[rows, 256 + head * 128 : 256 + (head + 1) * 128] = (
                a[0:CHUNK, 128:256] + b[0:CHUNK, 128:256]
            ).astype(bf16)
            dproj_ref[rows, 512 + head * 256 : 640 + head * 256] = recv_ref[ja, 0:CHUNK, 256:384]
            dproj_ref[rows, 640 + head * 256 : 768 + head * 256] = recv_ref[ja + 1, 0:CHUNK, 256:384]
            both = a[CHUNK : CHUNK + 8, 0:128] + b[CHUNK : CHUNK + 8, 0:128]
            total = jnp.sum(both[0:2], 0, keepdims=True)
            beta = jnp.where(row == head, total, beta)
        dproj_ref[rows, 1536:1664] = beta.T.astype(bf16)
    dproj_ref[:, 1024:1536] = glogit_ref[...]
    for y in range(4):
        value = mm_tn(mix_ref[:, y * 256 : (y + 1) * 256], dproj_ref[...]).astype(bf16)
        mine, other = core_split(value, core)
        mine_ref[y] = mine
        other_ref[y] = other


def call(kernel, outs, *args, scratch=(), in_specs=None, windowed=False, name=None):
    grid = {} if in_specs is None or not windowed else {"grid": (1,)}
    return pl.pallas_call(
        kernel,
        **grid,
        out_shape=[jax.ShapeDtypeStruct(shape, dtype) for shape, dtype in outs],
        in_specs=in_specs or [pl.BlockSpec(memory_space=pltpu.VMEM)] * len(args),
        out_specs=[pl.BlockSpec(memory_space=pltpu.VMEM)] * len(outs),
        scratch_shapes=list(scratch),
        compiler_params=pltpu.CompilerParams(vmem_limit_bytes=VMEM_LIMIT),
        name=name,
    )(*args)


def per_device(
    inputs,
    decay_rate,
    cotangent,
    mix_gain,
    query_weight,
    key_weight,
    value_weight,
    gate_weight,
    beta_weight,
    conv_query,
    conv_key,
    conv_value,
    out_gain,
    output_weight,
    ffn_gain,
    ffn_gate,
    ffn_up,
    ffn_down,
):
    y = lax.axis_index("batch")
    s = lax.axis_index("seq")
    x = lax.axis_index("tensor")
    z, core = s // 2, s % 2
    head, half = (s // 2) % 2, s % 2
    tokens = inputs.reshape(256, 1024)
    cot = cotangent.reshape(256, 1024)

    shard1 = jnp.concatenate(
        [
            query_weight,
            key_weight,
            value_weight,
            gate_weight,
            beta_weight,
            mix_gain[:, None],
            ffn_gain[:, None],
            jnp.zeros((32, W1_COLS - 1540), bf16),
        ],
        1,
    )
    part_a, part_b = shard1[:16], shard1[16:]
    group_a = jnp.stack([part_a] + [move_y(part_a, d) for d in (1, 2, 3)])
    group_b = jnp.stack([part_b] + [move_z(part_b, d) for d in (1, 2, 3)])
    own_a = [group_a] + [move_z(group_a, d) for d in (1, 2, 3)]
    own_b = [group_b] + [move_y(group_b, d) for d in (1, 2, 3)]
    sib_a = [move_core(v) for v in own_a]
    sib_b = [move_core(v) for v in own_b]

    fill = jnp.zeros((32, FFP - 704), bf16)
    shard2 = jnp.concatenate(
        [output_weight, ffn_gate, fill, ffn_up, fill, ffn_down, fill], 1
    )
    w2 = lax.all_gather(shard2, ("batch", "seq"), axis=0, tiled=True)

    logs = jnp.cumsum(jnp.log(decay_rate), 1).transpose(0, 2, 1)
    logs = jnp.broadcast_to(logs[:, :, None, :], (2, 2, 2, CHUNK)).reshape(8, CHUNK)
    logs = lax.all_to_all(logs, "seq", 0, 0)
    taps = jnp.concatenate(
        [
            lax.dynamic_slice_in_dim(conv_query, head * DK, DK, 0),
            lax.dynamic_slice_in_dim(conv_key, head * DK, DK, 0),
            lax.dynamic_slice_in_dim(conv_value, head * DV + half * HV, HV, 0),
        ],
        0,
    ).astype(f32)
    taps = jnp.pad(taps.T, ((0, 8 - KCONV), (0, 0)))
    gain_row = jnp.broadcast_to(out_gain.astype(f32)[None], (8, 2 * DV))
    own_tokens = pick(tokens.reshape(4, 64, 1024), x)
    cot4 = cot.reshape(4, 64, 1024)
    own_cot = pick(cot4, x)
    cot_turned = jnp.concatenate([pick(cot4, (x - d) % 4) for d in range(4)], 0)

    w1, mix_input, send, gate_logit, gains = call(
        project_kernel,
        [
            ((1024, W1_COLS), bf16),
            ((256, 1024), bf16),
            ((8, CHUNK_ROWS, CHAN), bf16),
            ((256, 512), f32),
            ((8, 1024), f32),
        ],
        *own_a,
        *own_b,
        *sib_a,
        *sib_b,
        tokens,
        scratch=[pltpu.SemaphoreType.DMA((64,))],
        in_specs=[pl.BlockSpec(memory_space=pl.ANY)] * 16 + [pl.BlockSpec(memory_space=pltpu.VMEM)],
        name="project",
    )
    recv = lax.all_to_all(send, "seq", 0, 0)
    square = ((NCHUNK, 128, 128), bf16)
    mixed, inv, wkeys, uvals, starts = call(
        forward_kernel,
        [square] * 5,
        recv,
        taps,
        logs,
        scratch=[pltpu.VMEM((16 + NCHUNK * CHUNK, CHAN), f32)],
        name="delta_forward",
    )
    mixed = lax.all_to_all(mixed, "seq", 0, 0)
    vm = pl.BlockSpec(memory_space=pltpu.VMEM)
    w_out_spec = pl.BlockSpec((1024, 512), lambda i: (0, 0))
    gated, part = call(
        output_kernel,
        [((256, 512), bf16), ((256, 1024), bf16)],
        mixed,
        gate_logit,
        gain_row,
        w2,
        in_specs=[vm, vm, vm, w_out_spec],
        windowed=True,
        name="output",
    )
    middle = own_tokens + scatter_x(part.reshape(4, 64, 1024), x)
    ffn_g = gains[1:2]
    r2 = lax.rsqrt(jnp.mean(middle * middle, -1, keepdims=True) + EPS)
    ffn_rows = (middle * r2 * ffn_g).astype(bf16)
    ffn_input = jnp.concatenate(gather_x(ffn_rows), 0)
    part, gpart, hidden, ggate, gup = call(
        ffn_kernel,
        [
            ((256, 1024), bf16),
            ((256, 1024), bf16),
            ((256, FFP), bf16),
            ((256, FFP), bf16),
            ((256, FFP), bf16),
        ],
        ffn_input,
        cot_turned,
        w2,
        name="ffn",
    )

    def scatter_turned(partial):
        blocks = partial.reshape(4, 64, 1024)
        got = [move_x(blocks[d], -d) for d in (1, 2, 3)]
        return blocks[0].astype(f32) + got[0].astype(f32) + got[1].astype(f32) + got[2].astype(f32)

    grad_ffn_input = scatter_turned(gpart)
    grad_ffn_w = jnp.concatenate(
        [mm_tn(ffn_input, ggate), mm_tn(ffn_input, gup), mm_tn(cot_turned, hidden)], 1
    ).astype(bf16)
    grad_ffn_w = lax.psum_scatter(
        grad_ffn_w, ("batch", "seq"), scatter_dimension=0, tiled=True
    ).astype(f32)
    result_rows = (middle + scatter_turned(part)).astype(bf16)
    result = in_order(gather_x(result_rows), x).astype(f32)

    v_r = middle * r2
    ffn_gain_sum = jnp.sum(grad_ffn_input * v_r, 0, keepdims=True)
    gg = grad_ffn_input * ffn_g
    grad_middle = own_cot.astype(f32) + r2 * (gg - v_r * jnp.mean(gg * v_r, -1, keepdims=True))
    grad_mix = in_order(gather_x(grad_middle.astype(bf16)), x).reshape(256, 1024)
    gmixed, glogit, ggain = call(
        output_back_kernel,
        [((8, CHUNK, 128), bf16), ((256, 512), bf16), ((8, 512), f32)],
        grad_mix,
        mixed,
        gate_logit,
        gain_row,
        w2,
        in_specs=[vm, vm, vm, vm, w_out_spec],
        windowed=True,
        name="output_back",
    )
    gmixed = lax.all_to_all(gmixed, "seq", 0, 0)
    grad_out_w = mm_tn(grad_mix, gated).astype(bf16).reshape(4, 4, 2, 2, 16, 512)
    first, second = grad_out_w[:, :, 0], grad_out_w[:, :, 1]
    grad_out_w = scatter_rows(
        jnp.where(core == 0, first, second), jnp.where(core == 0, second, first), y, z
    )
    gsend, gtaps = call(
        backward_kernel,
        [((8, CHUNK_ROWS, CHAN), bf16), ((8, CHAN), f32)],
        recv,
        taps,
        logs,
        gmixed,
        inv,
        wkeys,
        uvals,
        starts,
        scratch=[
            pltpu.VMEM((16 + NCHUNK * CHUNK, CHAN), f32),
            pltpu.VMEM((32 + NCHUNK * CHUNK, CHAN), f32),
        ],
        name="delta_backward",
    )
    grecv = lax.all_to_all(gsend, "seq", 0, 0)
    dproj, mine, other = call(
        project_back_kernel,
        [
            ((256, W1_COLS), bf16),
            ((4, 4, 2, 16, W1_COLS), bf16),
            ((4, 4, 2, 16, W1_COLS), bf16),
        ],
        grecv,
        glogit,
        mix_input,
        name="project_back",
    )
    part = mm_nt(dproj, w1).astype(bf16).reshape(4, 64, 1024)
    grad_mix_input = scatter_x(part, x)
    grad_w1 = scatter_rows(mine, other, y, z)

    mix_g = gains[0:1]
    r1 = lax.rsqrt(jnp.mean(own_tokens * own_tokens, -1, keepdims=True) + EPS)
    v_r = own_tokens * r1
    mix_gain_sum = jnp.sum(grad_mix_input * v_r, 0, keepdims=True)
    gg = grad_mix_input * mix_g
    grad_rows = grad_middle + r1 * (gg - v_r * jnp.mean(gg * v_r, -1, keepdims=True))
    grad_inputs = in_order(gather_x(grad_rows.astype(bf16)), x).astype(f32)

    gain_sums = sum4(jnp.concatenate([mix_gain_sum, ffn_gain_sum], 0), swap_x)
    tap_row = jnp.zeros((KCONV, 1024), f32)
    tap_row = lax.dynamic_update_slice(tap_row, gtaps[:KCONV, 0:128], (0, head * DK))
    tap_row = lax.dynamic_update_slice(tap_row, gtaps[:KCONV, 128:256], (0, 256 + head * DK))
    tap_row = lax.dynamic_update_slice(
        tap_row, gtaps[:KCONV, 256:384], (0, 512 + head * DV + half * HV)
    )
    small = jnp.concatenate(
        [tap_row, jnp.pad(ggain[0:1], ((0, 0), (0, 512))), gain_sums, jnp.zeros((1, 1024), f32)], 0
    )
    small = small + move_core(small)
    small = sum4(small, swap_z)
    small = sum4(small, swap_y)
    place = (y * 8 + s) * 32
    return (
        result.reshape(2, 128, 1024),
        grad_inputs.reshape(2, 128, 1024),
        lax.dynamic_slice(small[5], (place,), (32,)),
        grad_w1[:, 0:256],
        grad_w1[:, 256:512],
        grad_w1[:, 512:1024],
        grad_w1[:, 1024:1536],
        grad_w1[:, 1536:1538],
        small[:4, 0:256].T,
        small[:4, 256:512].T,
        small[:4, 512:1024].T,
        small[4, 0:512],
        grad_out_w,
        lax.dynamic_slice(small[6], (place,), (32,)),
        grad_ffn_w[:, 0:704],
        grad_ffn_w[:, FFP : FFP + 704],
        grad_ffn_w[:, 2 * FFP : 2 * FFP + 704],
    )


def solution(mesh):
    rows = ("batch", "seq")
    split = P(rows, "tensor")
    tokens = P("batch", "seq", None)
    taps = P("tensor", None)
    placed = (
        tokens,
        P("batch", "seq", "tensor"),
        tokens,
        P(rows),
        split,
        split,
        split,
        split,
        split,
        taps,
        taps,
        taps,
        P("tensor"),
        split,
        P(rows),
        split,
        split,
        split,
    )
    return jax.shard_map(
        per_device,
        mesh=mesh,
        in_specs=placed,
        out_specs=(
            tokens,
            tokens,
            P(rows),
            split,
            split,
            split,
            split,
            split,
            taps,
            taps,
            taps,
            P("tensor"),
            split,
            P(rows),
            split,
            split,
            split,
        ),
        check_vma=False,
    )
```

```python
from functools import partial

import jax
import jax.numpy as jnp
from jax import lax
from jax.experimental import pallas as pl
from jax.experimental.pallas import tpu as pltpu
from jax.sharding import PartitionSpec as P

bf16 = jnp.bfloat16
f32 = jnp.float32

DK = 128
DV = 256
HV = 128
KCONV = 4
CHUNK = 128
NCHUNK = 8
CHUNK_ROWS = CHUNK + 16
CHAN = 2 * DK + HV
W1_COLS = 1152
FF = 704
FFP = 768
FFN = 1024
W2_COLS = FFN + 3 * FFP
BETA = 1024
EPS = 1e-06
QF = DK ** (-0.5)
VMEM_LIMIT = 56 * 1024 * 1024
COST = 1000


def move_core(v):
    return lax.ppermute(v, "seq", [(i, i ^ 1) for i in range(8)])


def move_z(v, d):
    return lax.ppermute(v, "seq", [(i, (i + 2 * d) % 8) for i in range(8)])


def move_y(v, d):
    return lax.ppermute(v, "batch", [(i, (i + d) % 4) for i in range(4)])


def move_x(v, d):
    return lax.ppermute(v, "tensor", [(i, (i + d) % 4) for i in range(4)])


def pick(v, i):
    return lax.dynamic_index_in_dim(v, i, 0, keepdims=False)


def gather_x(rows):
    return [rows] + [move_x(rows, d) for d in (1, 2, 3)]


def mm(a, b):
    return jnp.dot(a.astype(bf16), b.astype(bf16), preferred_element_type=f32)


def mm_nt(a, b):
    return lax.dot_general(
        a.astype(bf16), b.astype(bf16), (((1,), (1,)), ((), ())), preferred_element_type=f32
    )


def mm_tn(a, b):
    return lax.dot_general(
        a.astype(bf16), b.astype(bf16), (((0,), (0,)), ((), ())), preferred_element_type=f32
    )


def halves(v):
    hi = v.astype(bf16)
    return hi, (v - hi.astype(f32)).astype(bf16)


def mm3(a, b):
    (ah, al), (bh, bl) = a, b
    return mm(ah, bh) + (mm(ah, bl) + mm(al, bh))


def sigmoid(v):
    return 1.0 / (1.0 + jnp.exp(-v))


def first_pack_kernel(q_ref, k_ref, v_ref, beta_ref, mix_ref, ffn_ref, out_ref):
    out_ref[:, 0:256] = q_ref[...]
    out_ref[:, 256:512] = k_ref[...]
    out_ref[:, 512:1024] = v_ref[...]
    row = lax.broadcasted_iota(jnp.int32, (128, 32), 0)
    last = jnp.zeros((128, 32), f32)
    beta = beta_ref[...].astype(f32)
    for place, part in enumerate(
        (beta[0:1], beta[1:2], mix_ref[...].astype(f32), ffn_ref[...].astype(f32))
    ):
        last = jnp.where(row == place, part, last)
    out_ref[:, BETA:W1_COLS] = last.T.astype(bf16)


def second_pack_kernel(out_w_ref, gate_ref, fgate_ref, fup_ref, fdown_ref, out_ref):
    out_ref[:, 0:512] = out_w_ref[...]
    out_ref[:, 512:1024] = gate_ref[...]
    for place, ref in enumerate((fgate_ref, fup_ref, fdown_ref)):
        first = FFN + place * FFP
        out_ref[:, first + 640 : first + FFP] = jnp.zeros((32, 128), bf16)
        out_ref[:, first : first + FF] = ref[...]


def project_kernel(*refs):
    own, sib = refs[0:4], refs[4:8]
    x_ref, l_ref = refs[8:10]
    w_ref, mix_ref, send_ref, gain_ref, sem = refs[10:]
    y = lax.axis_index("batch")
    s = lax.axis_index("seq")
    z, core = s // 2, s % 2
    copies = []
    for far in range(4):
        for near in range(4):
            first = ((y - far + 4) % 4) * 256 + ((z - near + 4) % 4) * 64
            for group, c in ((own, core), (sib, 1 - core)):
                row = pl.multiple_of(first + c * 32, 32)
                copies.append(
                    pltpu.make_async_copy(
                        group[far].at[near], w_ref.at[pl.ds(row, 32)], sem.at[len(copies)]
                    )
                )
    for copy in copies:
        copy.start()
    xs = x_ref[...]
    normed = xs * lax.rsqrt(jnp.mean(xs * xs, -1, keepdims=True) + EPS)
    for copy in copies:
        copy.wait()
    last = w_ref[:, BETA:W1_COLS]
    row = lax.broadcasted_iota(jnp.int32, (8, 128), 0)
    lane = lax.broadcasted_iota(jnp.int32, (8, 128), 1)
    chosen = jnp.where(lane == row + 2, 1.0, 0.0).astype(bf16)
    gains = mm_nt(chosen, last)
    gain_ref[...] = gains
    mix = (normed * gains[0:1]).astype(bf16)
    mix_ref[...] = mix
    q = mm(mix, w_ref[:, 0:256]).astype(bf16)
    k = mm(mix, w_ref[:, 256:512]).astype(bf16)
    v = mm(mix, w_ref[:, 512:1024]).astype(bf16)
    logit = lax.dot_general(last, mix, (((0,), (1,)), ((), ())), preferred_element_type=f32)
    row16 = lax.broadcasted_iota(jnp.int32, (16, 128), 0)
    for j in range(8):
        seq, head, u = j // 4, (j // 2) % 2, j % 2
        rows = slice(seq * CHUNK, (seq + 1) * CHUNK)
        send_ref[j, 0:CHUNK, 0:128] = q[rows, head * 128 : (head + 1) * 128]
        send_ref[j, 0:CHUNK, 128:256] = k[rows, head * 128 : (head + 1) * 128]
        first = head * DV + u * HV
        send_ref[j, 0:CHUNK, 256:384] = v[rows, first : first + HV]
        b = logit[head : head + 1, rows]
        b_hi = b.astype(bf16).astype(f32)
        logs = l_ref[2 * seq + head : 2 * seq + head + 1, :]
        l_hi = logs.astype(bf16).astype(f32)
        l_mid = (logs - l_hi).astype(bf16).astype(f32)
        tile = jnp.zeros((16, 128), f32)
        for place, part in enumerate((b_hi, b - b_hi, l_hi, l_mid, (logs - l_hi) - l_mid)):
            tile = jnp.where(row16 == place, part, tile)
        send_ref[j, CHUNK:CHUNK_ROWS, 0:128] = tile.astype(bf16)
        send_ref[j, CHUNK:CHUNK_ROWS, 128:384] = jnp.zeros((16, 256), bf16)


def gate_kernel(mix_ref, w_ref, gate_ref):
    gate_ref[...] = mm(mix_ref[...], w_ref[...])


def masks():
    i = lax.broadcasted_iota(jnp.int32, (CHUNK, CHUNK), 0)
    j = lax.broadcasted_iota(jnp.int32, (CHUNK, CHUNK), 1)
    return i, j


def inverses(systems, i, j):
    split = [halves(n) for n in systems]
    pair = (i >> 1) == (j >> 1)
    unit = jnp.where(i == j, 1.0, 0.0)
    out = [unit - jnp.where(pair, n, 0.0) for n in systems]
    for level in range(1, 7):
        corner = ((i >> (level + 1)) == (j >> (level + 1))) & ((i >> level) != (j >> level))
        zero = jnp.zeros((CHUNK, CHUNK), bf16)
        for c in range(len(systems)):
            below = tuple(jnp.where(corner, part, zero) for part in split[c])
            now = halves(out[c])
            out[c] = out[c] - mm3(halves(mm3(now, below)), now)
    return out


def row_parts(recv_ref):
    tiles = [recv_ref[c, CHUNK:CHUNK_ROWS, 0:128].astype(f32) for c in range(NCHUNK)]
    betas = jnp.concatenate([t[0:1] + t[1:2] for t in tiles], 0)
    logs = jnp.concatenate([(t[2:3] + t[3:4]) + t[4:5] for t in tiles], 0)
    return sigmoid(betas.T), logs


def load_tokens(recv_ref, ext):
    ext[0:16, :] = jnp.zeros((16, CHAN), f32)
    for c in range(NCHUNK):
        ext[16 + c * CHUNK : 16 + (c + 1) * CHUNK, :] = recv_ref[c, 0:CHUNK, :].astype(f32)


def convolve(ext, taps, c):
    first = 16 + c * CHUNK - (KCONV - 1)
    pre = ext[pl.ds(first, CHUNK), :] * taps[0:1]
    for tap in range(1, KCONV):
        pre = pre + ext[pl.ds(first + tap, CHUNK), :] * taps[tap : tap + 1]
    return pre


def unit(a):
    scale = lax.rsqrt(jnp.sum(a * a, -1, keepdims=True) + EPS)
    return a * scale, scale


def spread_of(lrows, lcols, c, i, j):
    gap = lcols[:, c : c + 1] - lrows[c : c + 1, :]
    return jnp.where(i >= j, jnp.exp(jnp.where(i >= j, gap, 0.0)), 0.0)


def forward_kernel(recv_ref, taps_ref, mixed_ref, inv_ref, w_ref, u_ref, s_ref, ext):
    load_tokens(recv_ref, ext)
    taps = taps_ref[...]
    betas, lrows = row_parts(recv_ref)
    lcols = lrows.T
    i, j = masks()
    strict = i > j
    qs, ks, kds, ps, systems, rights, grown = [], [], [], [], [], [], []
    for c in range(NCHUNK):
        pre = convolve(ext, taps, c)
        act = pre * sigmoid(pre)
        q = unit(act[:, 0:128])[0].astype(bf16)
        k = unit(act[:, 128:256])[0].astype(bf16)
        v = act[:, 256:384].astype(bf16)
        spread = spread_of(lrows, lcols, c, i, j)
        beta = betas[:, c : c + 1]
        lcol = lcols[:, c : c + 1]
        ltop = lrows[c : c + 1, CHUNK - 1 : CHUNK]
        grow = jnp.exp(lcol)
        kf = k.astype(f32)
        systems.append(jnp.where(strict, beta * spread * mm_nt(k, k), 0.0))
        ps.append((spread * mm_nt(q, k)).astype(bf16))
        rights.append(
            jnp.concatenate([beta * v.astype(f32), (beta * grow) * kf], 1).astype(bf16)
        )
        qs.append((grow * q.astype(f32)).astype(bf16))
        kds.append((jnp.exp(ltop - lcol) * kf).astype(bf16))
        grown.append(jnp.exp(ltop))
    inv = inverses(systems, i, j)
    us, ws = [], []
    for c in range(NCHUNK):
        low = inv[c].astype(bf16)
        inv_ref[c] = low
        both = mm(low, rights[c])
        us.append(both[:, 0:128])
        ws.append(both[:, 128:256].astype(bf16))
        w_ref[c] = ws[c]
    state = jnp.zeros((DK, HV), f32)
    for c in range(NCHUNK):
        start = state.astype(bf16)
        s_ref[c] = start
        u = (us[c] - mm(ws[c], start)).astype(bf16)
        u_ref[c] = u
        state = grown[c] * state + mm_tn(kds[c], u)
        mixed_ref[c] = (QF * (mm(qs[c], start) + mm(ps[c], u))).astype(bf16)


def backward_kernel(
    recv_ref, taps_ref, grad_ref, inv_ref, w_ref, u_ref, s_ref, out_ref, tap_ref, ext, gext
):
    load_tokens(recv_ref, ext)
    taps = taps_ref[...]
    betas, lrows = row_parts(recv_ref)
    lcols = lrows.T
    i, j = masks()
    strict = i > j
    gext[16 + NCHUNK * CHUNK :, :] = jnp.zeros((16, CHAN), f32)
    kept = []
    for c in range(NCHUNK):
        pre = convolve(ext, taps, c)
        sig = sigmoid(pre)
        act = pre * sig
        q = unit(act[:, 0:128])[0].astype(bf16)
        k = unit(act[:, 128:256])[0].astype(bf16)
        spread = spread_of(lrows, lcols, c, i, j)
        lcol = lcols[:, c : c + 1]
        ltop = lrows[c : c + 1, CHUNK - 1 : CHUNK]
        grow = jnp.exp(lcol)
        fade = jnp.exp(ltop - lcol)
        p = (spread * mm_nt(q, k)).astype(bf16)
        kd = (fade * k.astype(f32)).astype(bf16)
        grown_q = (QF * grow * q.astype(f32)).astype(bf16)
        g = grad_ref[c]
        du = QF * mm_tn(p, g)
        ds = mm_tn(grown_q, g)
        kept.append((q, k, grow, fade, jnp.exp(ltop), kd, du, ds))
    state = jnp.zeros((DK, HV), f32)
    after, dus = [None] * NCHUNK, [None] * NCHUNK
    for c in reversed(range(NCHUNK)):
        top, kd, du, ds = kept[c][4:]
        low = state.astype(bf16)
        after[c] = low
        du = (du + mm(kd, low)).astype(bf16)
        dus[c] = du
        state = top * state + ds - mm_tn(w_ref[c], du)
    cols = []
    for c in range(NCHUNK):
        q, k, grow, fade = kept[c][:4]
        beta = betas[:, c : c + 1]
        spread = spread_of(lrows, lcols, c, i, j)
        g = grad_ref[c]
        u = u_ref[c]
        start = s_ref[c]
        pre = convolve(ext, taps, c)
        sig = sigmoid(pre)
        act = pre * sig
        v = act[:, 256:384].astype(bf16).astype(f32)
        dr = mm_tn(inv_ref[c], dus[c])
        drl = dr.astype(bf16)
        dp = (QF * spread * mm_nt(g, u)).astype(bf16)
        dt = jnp.where(strict, -spread * mm_nt(drl, u), 0.0)
        dkk = (beta * dt).astype(bf16)
        recalled = grow * mm(k, start)
        cols.append(
            jnp.sum(dt * mm_nt(k, k), -1, keepdims=True)
            + jnp.sum(dr * (v - recalled), -1, keepdims=True)
        )
        dq = mm(dp, k) + (QF * grow) * mm_nt(g, start)
        dk = (
            mm_tn(dp, q)
            + fade * mm_nt(u, after[c])
            + (mm(dkk, k) + mm_tn(dkk, k))
            - (beta * grow) * mm_nt(drl, start)
        )
        dv = beta * dr
        slope = sig * (1.0 + pre * (1.0 - sig))
        for first, part in ((0, dq), (128, dk)):
            a = act[:, first : first + 128]
            n, scale = unit(a)
            da = scale * (part - n * jnp.sum(n * part, -1, keepdims=True))
            gext[16 + c * CHUNK : 16 + (c + 1) * CHUNK, first : first + 128] = (
                da * slope[:, first : first + 128]
            )
        gext[16 + c * CHUNK : 16 + (c + 1) * CHUNK, 256:384] = dv * slope[:, 256:384]
    dbeta = jnp.concatenate(cols, 1) * betas * (1.0 - betas)
    brows = dbeta.T
    row16 = lax.broadcasted_iota(jnp.int32, (16, 128), 0)
    tap_sums = [jnp.zeros((1, CHAN), f32) for _ in range(KCONV)]
    for c in range(NCHUNK):
        here = 16 + c * CHUNK
        gpre = gext[here : here + CHUNK, :]
        total = gpre * taps[KCONV - 1 : KCONV]
        tap_sums[KCONV - 1] = tap_sums[KCONV - 1] + jnp.sum(
            gpre * ext[here : here + CHUNK, :], 0, keepdims=True
        )
        for tap in range(KCONV - 1):
            back = KCONV - 1 - tap
            total = total + gext[pl.ds(here + back, CHUNK), :] * taps[tap : tap + 1]
            tap_sums[tap] = tap_sums[tap] + jnp.sum(
                gpre * ext[pl.ds(here - back, CHUNK), :], 0, keepdims=True
            )
        out_ref[c, 0:CHUNK, :] = total.astype(bf16)
        b = brows[c : c + 1, :]
        hi = b.astype(bf16).astype(f32)
        tile = jnp.where(row16 == 0, hi, jnp.where(row16 == 1, b - hi, 0.0))
        out_ref[c, CHUNK:CHUNK_ROWS, 0:128] = tile.astype(bf16)
        out_ref[c, CHUNK:CHUNK_ROWS, 128:384] = jnp.zeros((16, 256), bf16)
    tap_ref[...] = jnp.concatenate(tap_sums + [jnp.zeros((8 - KCONV, CHAN), f32)], 0)


def head_parts(mixed_ref, gate_ref, gain, seq, head):
    a = mixed_ref[4 * seq + 2 * head].astype(f32)
    b = mixed_ref[4 * seq + 2 * head + 1].astype(f32)
    mean = (jnp.sum(a * a, -1, keepdims=True) + jnp.sum(b * b, -1, keepdims=True)) / DV
    scale = lax.rsqrt(mean + EPS)
    logit = gate_ref[seq * CHUNK : (seq + 1) * CHUNK, head * DV : (head + 1) * DV]
    n = jnp.concatenate([a, b], 1) * scale
    return n, scale, logit, sigmoid(logit), gain[:, head * DV : (head + 1) * DV]


def send_in_order(part_ref, outs):
    x = lax.axis_index("tensor")
    for d, out in enumerate(outs):
        out[...] = part_ref[pl.ds(pl.multiple_of(((x + d) % 4) * 64, 64), 64), :]


def output_kernel(mixed_ref, gate_ref, gain_ref, w_ref, gated_ref, o0, o1, o2, o3, part_ref):
    gain = gain_ref[0:1, :]
    for seq in range(2):
        for head in range(2):
            n, _, logit, sig, own = head_parts(mixed_ref, gate_ref, gain, seq, head)
            gated_ref[seq * CHUNK : (seq + 1) * CHUNK, head * DV : (head + 1) * DV] = (
                n * own * (logit * sig)
            ).astype(bf16)
    part_ref[...] = mm_nt(gated_ref[...], w_ref[...]).astype(bf16)
    send_in_order(part_ref, (o0, o1, o2, o3))


def middle_kernel(o0, o1, o2, o3, x_ref, gain_ref, middle_ref, rows_ref):
    middle = x_ref[...] + added(o0, o1, o2, o3)
    middle_ref[...] = middle
    scale = lax.rsqrt(jnp.mean(middle * middle, -1, keepdims=True) + EPS)
    rows_ref[...] = (middle * scale * gain_ref[1:2, :]).astype(bf16)


def norm_back(g, v, gain):
    scale = lax.rsqrt(jnp.mean(v * v, -1, keepdims=True) + EPS)
    n = v * scale
    gg = g * gain
    return scale * (gg - n * jnp.mean(gg * n, -1, keepdims=True)), jnp.sum(g * n, 0, keepdims=True)


def added(o0, o1, o2, o3):
    return (o0[...].astype(f32) + o1[...].astype(f32)) + (o2[...].astype(f32) + o3[...].astype(f32))


def ffn_back_kernel(g0, g1, g2, g3, middle_ref, cot_ref, gain_ref, grad_ref, rows_ref, sum_ref):
    part, gain_sum = norm_back(added(g0, g1, g2, g3), middle_ref[...], gain_ref[1:2, :])
    grad = cot_ref[...].astype(f32) + part
    grad_ref[...] = grad
    rows_ref[...] = grad.astype(bf16)
    sum_ref[...] = jnp.broadcast_to(gain_sum, sum_ref.shape)


def result_kernel(o0, o1, o2, o3, middle_ref, rows_ref):
    rows_ref[...] = (middle_ref[...] + added(o0, o1, o2, o3)).astype(bf16)


def first_back_kernel(o0, o1, o2, o3, x_ref, grad_ref, gain_ref, out_ref):
    parts = [o[...].astype(f32) for o in (o1, o2, o3)]
    a, b, c = turned(parts, lax.axis_index("tensor"))
    part, _ = norm_back((o0[...].astype(f32) + a) + (b + c), x_ref[...], gain_ref[0:1, :])
    out_ref[...] = grad_ref[...].astype(f32) + part


def place_rows(blocks, out_ref):
    x = lax.axis_index("tensor")
    for d, block in enumerate(blocks):
        row = pl.multiple_of(((x - d + 4) % 4) * 64, 64)
        out_ref[pl.ds(row, 64), :] = block.astype(out_ref.dtype)


def place_kernel(c0, c1, c2, c3, out_ref):
    place_rows([c[...] for c in (c0, c1, c2, c3)], out_ref)


def output_back_kernel(
    c0, c1, c2, c3, mixed_ref, gate_ref, gain_ref, w_ref, gmix_ref, gmixed_ref, glogit_ref, ggain_ref
):
    place_rows([c[...] for c in (c0, c1, c2, c3)], gmix_ref)
    gain = gain_ref[0:1, :]
    grad = mm(gmix_ref[...], w_ref[...])
    sums = []
    for head in range(2):
        total = jnp.zeros((1, DV), f32)
        for seq in range(2):
            n, scale, logit, sig, own = head_parts(mixed_ref, gate_ref, gain, seq, head)
            g = grad[seq * CHUNK : (seq + 1) * CHUNK, head * DV : (head + 1) * DV]
            t = g * (logit * sig)
            total = total + jnp.sum(t * n, 0, keepdims=True)
            gn = t * own
            gm = scale * (gn - n * jnp.mean(gn * n, -1, keepdims=True))
            gmixed_ref[4 * seq + 2 * head] = gm[:, 0:128].astype(bf16)
            gmixed_ref[4 * seq + 2 * head + 1] = gm[:, 128:256].astype(bf16)
            slope = sig * (1.0 + logit * (1.0 - sig))
            glogit_ref[seq * CHUNK : (seq + 1) * CHUNK, head * DV : (head + 1) * DV] = (
                g * n * own * slope
            ).astype(bf16)
        sums.append(total)
    ggain_ref[...] = jnp.broadcast_to(jnp.concatenate(sums, 1), (8, 2 * DV))


def ffn_kernel(
    r0, r1, r2, r3, cot_ref, w_hbm, g0, g1, g2, g3, p0, p1, p2, p3, hidden_ref, ggate_ref, gup_ref,
    in_ref, w_ref, sem,
):
    copies = [
        pltpu.make_async_copy(
            w_hbm.at[:, pl.ds(FFN + i * FFP, FFP)], w_ref.at[i], sem.at[i]
        )
        for i in range(3)
    ]
    for copy in copies:
        copy.start()
    for d, ref in enumerate((r0, r1, r2, r3)):
        in_ref[d * 64 : (d + 1) * 64, :] = ref[...]
    tokens = in_ref[...]
    copies[0].wait()
    gate = mm(tokens, w_ref[0])
    copies[1].wait()
    up = mm(tokens, w_ref[1])
    copies[2].wait()
    ghidden = mm(cot_ref[...], w_ref[2])
    sig = sigmoid(gate)
    silu = gate * sig
    ggate = (ghidden * up * (sig * (1.0 + gate * (1.0 - sig)))).astype(bf16)
    gup = (ghidden * silu).astype(bf16)
    hidden = (silu * up).astype(bf16)
    hidden_ref[...] = hidden
    ggate_ref[...] = ggate
    gup_ref[...] = gup
    gpart = (mm_nt(ggate, w_ref[0]) + mm_nt(gup, w_ref[1])).astype(bf16)
    part = mm_nt(hidden, w_ref[2]).astype(bf16)
    for d in range(4):
        (g0, g1, g2, g3)[d][...] = gpart[d * 64 : (d + 1) * 64]
        (p0, p1, p2, p3)[d][...] = part[d * 64 : (d + 1) * 64]


def ffn_weight_kernel(
    r0, r1, r2, r3, cot_ref, hidden_ref, ggate_ref, gup_ref, out_hbm, in_ref, part_ref, sem
):
    for d, ref in enumerate((r0, r1, r2, r3)):
        in_ref[d * 64 : (d + 1) * 64, :] = ref[...]
    copies = []
    for i, (left, right) in enumerate(
        ((in_ref, ggate_ref), (in_ref, gup_ref), (cot_ref, hidden_ref))
    ):
        part_ref[i] = mm_tn(left[...], right[...]).astype(bf16)
        copies.append(
            pltpu.make_async_copy(
                part_ref.at[i], out_hbm.at[:, pl.ds(FFN + i * FFP, FFP)], sem.at[i]
            )
        )
        copies[i].start()
    for copy in copies:
        copy.wait()


def early_kernel(
    gmix_ref, gated_ref, mix_ref, glogit_ref, w_ref, given, part_ref, out_hbm, sum_ref, sem
):
    copies = []
    for i, (left, right) in enumerate(((gmix_ref, gated_ref), (mix_ref, glogit_ref))):
        sum_ref[i] = mm_tn(left[...], right[...]).astype(bf16)
        copies.append(
            pltpu.make_async_copy(sum_ref.at[i], out_hbm.at[:, pl.ds(i * 512, 512)], sem.at[i])
        )
        copies[i].start()
    part_ref[...] = mm_nt(glogit_ref[...], w_ref[...])
    for copy in copies:
        copy.wait()


def second_split_kernel(in_ref, out_ref, gate_ref, a_ref, b_ref, c_ref):
    out_ref[...] = in_ref[:, 0:512].astype(f32)
    gate_ref[...] = in_ref[:, 512:1024].astype(f32)
    for i, ref in enumerate((a_ref, b_ref, c_ref)):
        ref[...] = in_ref[:, FFN + i * FFP : FFN + i * FFP + FF].astype(f32)


def core_split(value, core, mine_ref, other_ref, y):
    value = value.reshape(4, 2, 32, value.shape[-1])
    first, second = value[:, 0], value[:, 1]
    mine = jnp.where(core == 0, first, second)
    other = jnp.where(core == 0, second, first)
    rows = slice(y * 128, (y + 1) * 128)
    mine_ref[rows, :] = mine.reshape(128, W1_COLS)
    other_ref[rows, :] = other.reshape(128, W1_COLS)


def coded(small):
    hi = small.astype(bf16).astype(f32)
    lo = (small - hi).astype(bf16).astype(f32)
    tile = jnp.concatenate([hi, lo], 0)
    tile = jnp.concatenate([tile, jnp.zeros((16, W1_COLS - 1024), f32)], 1)
    return tile.astype(bf16), hi + lo


def decoded(tile):
    tile = tile[:, 0:1024].astype(f32)
    return tile[0:8] + tile[8:16]


def project_back_kernel(
    recv_ref,
    mix_ref,
    gate_part_ref,
    w_ref,
    x_ref,
    taps_ref,
    ggain_ref,
    fgain_ref,
    part_ref,
    mine_ref,
    other_ref,
    small_ref,
    dproj_ref,
    row_ref,
):
    s = lax.axis_index("seq")
    core, head_here = s % 2, (s // 2) % 2
    row = lax.broadcasted_iota(jnp.int32, (128, 128), 0)
    for seq in range(2):
        rows = slice(seq * CHUNK, (seq + 1) * CHUNK)
        beta = jnp.zeros((128, 128), f32)
        for head in range(2):
            ja = 4 * seq + 2 * head
            a, b = recv_ref.at[ja], recv_ref.at[ja + 1]
            for first in (0, 128):
                total = a[0:CHUNK, first : first + 128].astype(f32) + b[
                    0:CHUNK, first : first + 128
                ].astype(f32)
                place = 2 * first + head * 128
                dproj_ref[rows, place : place + 128] = total.astype(bf16)
            dproj_ref[rows, 512 + head * 256 : 640 + head * 256] = a[0:CHUNK, 256:384]
            dproj_ref[rows, 640 + head * 256 : 768 + head * 256] = b[0:CHUNK, 256:384]
            both = a[CHUNK:CHUNK_ROWS, 0:128].astype(f32) + b[CHUNK:CHUNK_ROWS, 0:128].astype(f32)
            beta = jnp.where(row == head, both[0:1] + both[1:2], beta)
        dproj_ref[rows, BETA:W1_COLS] = beta.T.astype(bf16)
    part = mm_nt(dproj_ref[...], w_ref[...]) + gate_part_ref[...]
    part_ref[...] = part.astype(bf16)
    xs = x_ref[...]
    mix_sum = jnp.sum(
        part * (xs * lax.rsqrt(jnp.mean(xs * xs, -1, keepdims=True) + EPS)), 0, keepdims=True
    )
    row_ref[...] = jnp.zeros((8, 1024), f32)
    for first, base in (
        (0, head_here * 128),
        (128, 256 + head_here * 128),
        (256, 512 + head_here * 256 + core * 128),
    ):
        lanes = pl.ds(pl.multiple_of(base, 128), 128)
        row_ref[0:8, lanes] = taps_ref[0:8, first : first + 128]
    row_ref[4:5, 0:512] = ggain_ref[0:1, :]
    row_ref[5:6, :] = mix_sum
    row_ref[6:7, :] = fgain_ref[0:1, :]
    tile, value = coded(row_ref[...])
    small_ref[...] = value
    other_ref[512:528, :] = tile
    for y in range(4):
        value = mm_tn(mix_ref[:, y * 256 : (y + 1) * 256], dproj_ref[...]).astype(bf16)
        core_split(value, core, mine_ref, other_ref, y)


def turned(got, index):
    even = index % 2 == 0
    return jnp.where(even, got[2], got[0]), got[1], jnp.where(even, got[0], got[2])


def fold_kernel(axis, base_ref, *refs):
    count = 1 if axis == "batch" else 3
    got, small_ref, outs, small_out = refs[:count], refs[count], refs[count + 1 : -1], refs[-1]
    y, z = lax.axis_index("batch"), lax.axis_index("seq") // 2
    here = y if axis == "batch" else z
    size = outs[0].shape[0]
    parts = [decoded(g[4 * size : 4 * size + 16, :]) for g in got]
    if count == 1:
        small = small_ref[...] + parts[0]
    else:
        a, b, c = turned(parts, y)
        small = (small_ref[...] + a) + (b + c)
    tile, value = coded(small)
    small_out[...] = value
    for d, out in enumerate(outs):
        rows = pl.ds(pl.multiple_of(((here + d) % 4) * size, 32), size)
        total = base_ref[rows, :].astype(f32)
        for g in got:
            total = total + g[rows, :].astype(f32)
        out[0:size, :] = total.astype(out.dtype)
        if d > 0:
            out[size : size + 16, :] = tile


def first_out_kernel(
    base_ref, g1, g2, g3, small_ref,
    q_ref, k_ref, v_ref, beta_ref, tap_q_ref, tap_k_ref, tap_v_ref, out_gain_ref, gain_ref,
):
    got = (g1, g2, g3)
    total = base_ref[...]
    for g in got:
        total = total + g[0:32, :].astype(f32)
    q_ref[...] = total[:, 0:256]
    k_ref[...] = total[:, 256:512]
    v_ref[...] = total[:, 512:1024]
    beta_ref[...] = total[:, BETA:W1_COLS].T[0:2, :]
    a, b, c = turned([decoded(g[32:48, :]) for g in got], lax.axis_index("seq") // 2)
    small = (small_ref[...] + a) + (b + c)
    tap_q_ref[...] = small[0:4, 0:256]
    tap_k_ref[...] = small[0:4, 256:512]
    tap_v_ref[...] = small[0:4, 512:1024]
    out_gain_ref[...] = small[4:5, 0:512]
    place = (lax.axis_index("batch") * 8 + lax.axis_index("seq")) * 32
    gain_ref[...] = pltpu.roll(small, (1024 - place) % 1024, 1)[:, 0:128]


def gain_kernel(g0, g1, g2, g3, mix_ref, ffn_ref):
    a, b, c = turned([g1[...], g2[...], g3[...]], lax.axis_index("tensor"))
    total = (g0[...] + a) + (b + c)
    mix_ref[...] = total[5:6, 0:32]
    ffn_ref[...] = total[6:7, 0:32]


vmem = pl.BlockSpec(memory_space=pltpu.VMEM)
hbm = pl.BlockSpec(memory_space=pl.ANY)


def call(kernel, outs, *args, scratch=(), in_specs=None, out_specs=None, windowed=False, alias=None, name=None):
    grid = {"grid": (1,)} if windowed else {}
    return pl.pallas_call(
        kernel,
        **grid,
        out_shape=[jax.ShapeDtypeStruct(shape, dtype) for shape, dtype in outs],
        in_specs=in_specs or [vmem] * len(args),
        out_specs=out_specs or [vmem] * len(outs),
        input_output_aliases=alias or {},
        scratch_shapes=list(scratch),
        compiler_params=pltpu.CompilerParams(vmem_limit_bytes=VMEM_LIMIT),
        cost_estimate=pl.CostEstimate(flops=COST, bytes_accessed=COST, transcendentals=0),
        name=name,
    )(*args)


def fold(axis, base, got, small, size, name):
    outs = [((size, W1_COLS), f32)] + [((size + 16, W1_COLS), bf16)] * 3 + [((8, 1024), f32)]
    *out, small = call(partial(fold_kernel, axis), outs, base, *got, small, name=name)
    return out, small


def per_device(
    inputs,
    decay_rate,
    cotangent,
    mix_gain,
    query_weight,
    key_weight,
    value_weight,
    gate_weight,
    beta_weight,
    conv_query,
    conv_key,
    conv_value,
    out_gain,
    output_weight,
    ffn_gain,
    ffn_gate,
    ffn_up,
    ffn_down,
):
    s = lax.axis_index("seq")
    x = lax.axis_index("tensor")
    head, half = (s // 2) % 2, s % 2
    tokens = inputs.reshape(256, 1024)
    cot = cotangent.reshape(256, 1024)

    (shard1,) = call(
        first_pack_kernel,
        [((32, W1_COLS), bf16)],
        query_weight,
        key_weight,
        value_weight,
        beta_weight.T,
        mix_gain[None],
        ffn_gain[None],
        name="first_pack",
    )
    column = jnp.stack([shard1] + [move_z(shard1, d) for d in (1, 2, 3)])

    output_weight, column = lax.optimization_barrier((output_weight, column))
    (shard2,) = call(
        second_pack_kernel,
        [((32, W2_COLS), bf16)],
        output_weight,
        gate_weight,
        ffn_gate,
        ffn_up,
        ffn_down,
        name="second_pack",
    )
    own = [column] + [move_y(column, d) for d in (1, 2, 3)]
    sib = [move_core(v) for v in own]
    w2 = lax.all_gather(shard2, ("batch", "seq"), axis=0, tiled=True)

    logs = jnp.cumsum(jnp.log(decay_rate), 1).transpose(0, 2, 1).reshape(4, CHUNK)
    logs = jnp.pad(logs, ((0, 4), (0, 0)))
    taps = jnp.concatenate(
        [
            lax.dynamic_slice_in_dim(conv_query.T, head * DK, DK, 1),
            lax.dynamic_slice_in_dim(conv_key.T, head * DK, DK, 1),
            lax.dynamic_slice_in_dim(conv_value.T, head * DV + half * HV, HV, 1),
        ],
        1,
    ).astype(f32)
    taps = jnp.pad(taps, ((0, 8 - KCONV), (0, 0)))
    gain_row = jnp.broadcast_to(out_gain.astype(f32)[None], (8, 2 * DV))
    own_tokens = pick(tokens.reshape(4, 64, 1024), x)
    cot4 = cot.reshape(4, 64, 1024)
    own_cot = pick(cot4, x)
    cot_turned = jnp.concatenate([pick(cot4, (x - d) % 4) for d in range(4)], 0)

    w1, mix_input, send, gains = call(
        project_kernel,
        [
            ((1024, W1_COLS), bf16),
            ((256, 1024), bf16),
            ((8, CHUNK_ROWS, CHAN), bf16),
            ((8, 1024), f32),
        ],
        *own,
        *sib,
        tokens,
        logs,
        scratch=[pltpu.SemaphoreType.DMA((32,))],
        in_specs=[hbm] * 8 + [vmem] * 2,
        name="project",
    )
    recv = lax.all_to_all(send, "seq", 0, 0)
    square = ((NCHUNK, 128, 128), bf16)
    mixed, inv, wkeys, uvals, starts = call(
        forward_kernel,
        [square] * 5,
        recv,
        taps,
        scratch=[pltpu.VMEM((16 + NCHUNK * CHUNK, CHAN), f32)],
        name="delta_forward",
    )
    mixed = lax.all_to_all(mixed, "seq", 0, 0)
    out_w = pl.BlockSpec((1024, 512), lambda i: (0, 0))
    gate_w = pl.BlockSpec((1024, 512), lambda i: (0, 1))
    (gate_logit,) = call(
        gate_kernel,
        [((256, 512), f32)],
        mix_input,
        w2,
        in_specs=[vmem, gate_w],
        windowed=True,
        name="gate",
    )
    quarter = ((64, 1024), bf16)
    gated, *pieces = call(
        output_kernel,
        [((256, 512), bf16)] + [quarter] * 4,
        mixed,
        gate_logit,
        gain_row,
        w2,
        in_specs=[vmem] * 3 + [out_w],
        scratch=[pltpu.VMEM((256, 1024), bf16)],
        windowed=True,
        name="output",
    )
    middle, ffn_rows = call(
        middle_kernel,
        [((64, 1024), f32), quarter],
        pieces[0],
        *[move_x(pieces[d], d) for d in (1, 2, 3)],
        own_tokens,
        gains,
        name="middle",
    )
    ffn_blocks = gather_x(ffn_rows)
    hidden_shape = ((256, FFP), bf16)
    ffn_out = call(
        ffn_kernel,
        [quarter] * 8 + [hidden_shape] * 3,
        *ffn_blocks,
        cot_turned,
        w2,
        in_specs=[vmem] * 5 + [hbm],
        scratch=[
            pltpu.VMEM((256, 1024), bf16),
            pltpu.VMEM((3, 1024, FFP), bf16),
            pltpu.SemaphoreType.DMA((3,)),
        ],
        name="ffn",
    )
    gpieces, rpieces, (hidden, ggate, gup) = ffn_out[:4], ffn_out[4:8], ffn_out[8:]
    got = [move_x(gpieces[d], -d) for d in (1, 2, 3)]
    (grad_w2,) = call(
        ffn_weight_kernel,
        [((1024, W2_COLS), bf16)],
        *ffn_blocks,
        cot_turned,
        hidden,
        ggate,
        gup,
        out_specs=[hbm],
        scratch=[
            pltpu.VMEM((256, 1024), bf16),
            pltpu.VMEM((3, 1024, FFP), bf16),
            pltpu.SemaphoreType.DMA((3,)),
        ],
        name="ffn_weight",
    )
    middle, grad_w2 = lax.optimization_barrier((middle, grad_w2))
    grad_middle, grad_rows, ffn_gain_sum = call(
        ffn_back_kernel,
        [((64, 1024), f32), quarter, ((8, 1024), f32)],
        gpieces[0],
        *got,
        middle,
        own_cot,
        gains,
        name="ffn_back",
    )
    mix_blocks = gather_x(grad_rows)
    grad_mix, gmixed, glogit, ggain = call(
        output_back_kernel,
        [((256, 1024), bf16), ((8, CHUNK, 128), bf16), ((256, 512), bf16), ((8, 512), f32)],
        *mix_blocks,
        mixed,
        gate_logit,
        gain_row,
        w2,
        in_specs=[vmem] * 7 + [out_w],
        windowed=True,
        name="output_back",
    )
    rpieces, gmixed = lax.optimization_barrier((tuple(rpieces), gmixed))
    gmixed = lax.all_to_all(gmixed, "seq", 0, 0)
    rgot = [move_x(rpieces[d], -d) for d in (1, 2, 3)]
    gate_part, grad_w2 = call(
        early_kernel,
        [((256, 1024), f32), ((1024, W2_COLS), bf16)],
        grad_mix,
        gated,
        mix_input,
        glogit,
        w2,
        grad_w2,
        in_specs=[vmem] * 4 + [gate_w, hbm],
        out_specs=[vmem, hbm],
        scratch=[pltpu.VMEM((2, 1024, 512), bf16), pltpu.SemaphoreType.DMA((2,))],
        windowed=True,
        alias={5: 1},
        name="early",
    )
    grad_w2 = lax.psum_scatter(grad_w2, ("batch", "seq"), scatter_dimension=0, tiled=True)
    gsend, gtaps = call(
        backward_kernel,
        [((8, CHUNK_ROWS, CHAN), bf16), ((8, CHAN), f32)],
        recv,
        taps,
        gmixed,
        inv,
        wkeys,
        uvals,
        starts,
        scratch=[
            pltpu.VMEM((16 + NCHUNK * CHUNK, CHAN), f32),
            pltpu.VMEM((32 + NCHUNK * CHUNK, CHAN), f32),
        ],
        name="delta_backward",
    )
    gsend, rgot = lax.optimization_barrier((gsend, tuple(rgot)))
    (result_rows,) = call(result_kernel, [quarter], rpieces[0], *rgot, middle, name="result_rows")
    grecv = lax.all_to_all(gsend, "seq", 0, 0)
    (result,) = call(place_kernel, [((256, 1024), f32)], *gather_x(result_rows), name="result")
    grecv, result = lax.optimization_barrier((grecv, result))
    part, mine, other, small = call(
        project_back_kernel,
        [
            ((256, 1024), bf16),
            ((512, W1_COLS), bf16),
            ((528, W1_COLS), bf16),
            ((8, 1024), f32),
        ],
        grecv,
        mix_input,
        gate_part,
        w1,
        tokens,
        gtaps,
        ggain,
        ffn_gain_sum,
        scratch=[
            pltpu.VMEM((256, W1_COLS), bf16),
            pltpu.VMEM((8, 1024), f32),
        ],
        name="project_back",
    )
    out, small = fold("batch", mine, [move_core(other)], small, 128, "first_core")
    got = [move_y(out[d], d) for d in (1, 2, 3)]
    parts = gather_x(part)
    out, small = fold("seq", out[0], got, small, 32, "first_y")
    got = [move_z(out[d], d) for d in (1, 2, 3)]
    grad_q, grad_k, grad_v, grad_beta, tap_q, tap_k, tap_v, grad_out_gain, gain_rows = call(
        first_out_kernel,
        [
            ((32, 256), f32),
            ((32, 256), f32),
            ((32, 512), f32),
            ((2, 32), f32),
            ((4, 256), f32),
            ((4, 256), f32),
            ((4, 512), f32),
            ((1, 512), f32),
            ((8, 128), f32),
        ],
        out[0],
        *got,
        small,
        name="first_z",
    )
    (grad_inputs,) = call(
        first_back_kernel,
        [((256, 1024), f32)],
        *parts,
        tokens,
        grad_mix,
        gains,
        name="first_back",
    )
    grad_mix_gain, grad_ffn_gain = call(
        gain_kernel, [((1, 32), f32)] * 2, *gather_x(gain_rows), name="gain_sums"
    )
    grad_out_w, grad_gate_w, grad_fgate, grad_fup, grad_fdown = call(
        second_split_kernel,
        [((32, 512), f32)] * 2 + [((32, FF), f32)] * 3,
        grad_w2,
        name="second_split",
    )
    return (
        result.reshape(2, 128, 1024),
        grad_inputs.reshape(2, 128, 1024),
        grad_mix_gain[0],
        grad_q,
        grad_k,
        grad_v,
        grad_gate_w,
        grad_beta.T,
        tap_q.T,
        tap_k.T,
        tap_v.T,
        grad_out_gain[0],
        grad_out_w,
        grad_ffn_gain[0],
        grad_fgate,
        grad_fup,
        grad_fdown,
    )


def solution(mesh):
    rows = ("batch", "seq")
    split = P(rows, "tensor")
    tokens = P("batch", "seq", None)
    taps = P("tensor", None)
    placed = (
        tokens,
        P("batch", "seq", "tensor"),
        tokens,
        P(rows),
        split,
        split,
        split,
        split,
        split,
        taps,
        taps,
        taps,
        P("tensor"),
        split,
        P(rows),
        split,
        split,
        split,
    )
    return jax.shard_map(
        per_device,
        mesh=mesh,
        in_specs=placed,
        out_specs=(
            tokens,
            tokens,
            P(rows),
            split,
            split,
            split,
            split,
            split,
            taps,
            taps,
            taps,
            P("tensor"),
            split,
            P(rows),
            split,
            split,
            split,
        ),
        check_vma=False,
    )
```

```python
from functools import partial

import jax
import jax.numpy as jnp
from jax import lax
from jax.experimental import pallas as pl
from jax.experimental.pallas import tpu as pltpu
from jax.sharding import PartitionSpec as P

bf16 = jnp.bfloat16
f32 = jnp.float32

DK = 128
DV = 256
HV = 128
KCONV = 4
CHUNK = 128
NCHUNK = 8
CHUNK_ROWS = CHUNK + 16
CHAN = 2 * DK + HV
W1_COLS = 1152
FF = 704
FFP = 768
FFN = 1024
W2_COLS = FFN + 3 * FFP
BETA = 1024
EPS = 1e-06
QF = DK ** (-0.5)
COST = 1000


def move_core(v):
    return lax.ppermute(v, "seq", [(i, i ^ 1) for i in range(8)])


def move_z(v, d):
    return lax.ppermute(v, "seq", [(i, (i + 2 * d) % 8) for i in range(8)])


def move_y(v, d):
    return lax.ppermute(v, "batch", [(i, (i + d) % 4) for i in range(4)])


def move_x(v, d):
    return lax.ppermute(v, "tensor", [(i, (i + d) % 4) for i in range(4)])


def pick(v, i):
    return lax.dynamic_index_in_dim(v, i, 0, keepdims=False)


def gather_x(rows):
    return [rows] + [move_x(rows, d) for d in (1, 2, 3)]


def mm(a, b):
    return jnp.dot(a.astype(bf16), b.astype(bf16), preferred_element_type=f32)


def mm_nt(a, b):
    return lax.dot_general(
        a.astype(bf16), b.astype(bf16), (((1,), (1,)), ((), ())), preferred_element_type=f32
    )


def mm_tn(a, b):
    return lax.dot_general(
        a.astype(bf16), b.astype(bf16), (((0,), (0,)), ((), ())), preferred_element_type=f32
    )


def sigmoid(v):
    return 1.0 / (1.0 + jnp.exp(-v))


def first_pack_kernel(q_ref, k_ref, v_ref, beta_ref, mix_ref, ffn_ref, out_ref):
    out_ref[:, 0:256] = q_ref[...]
    out_ref[:, 256:512] = k_ref[...]
    out_ref[:, 512:1024] = v_ref[...]
    row = lax.broadcasted_iota(jnp.int32, (128, 32), 0)
    last = jnp.zeros((128, 32), f32)
    beta = beta_ref[...].astype(f32)
    for place, part in enumerate(
        (beta[0:1], beta[1:2], mix_ref[...].astype(f32), ffn_ref[...].astype(f32))
    ):
        last = jnp.where(row == place, part, last)
    out_ref[:, BETA:W1_COLS] = last.T.astype(bf16)


def second_pack_kernel(out_w_ref, gate_ref, fgate_ref, fup_ref, fdown_ref, out_ref):
    out_ref[:, 0:512] = out_w_ref[...]
    out_ref[:, 512:1024] = gate_ref[...]
    for place, ref in enumerate((fgate_ref, fup_ref, fdown_ref)):
        first = FFN + place * FFP
        out_ref[:, first + 640 : first + FFP] = jnp.zeros((32, 128), bf16)
        out_ref[:, first : first + FF] = ref[...]


def project_kernel(*refs):
    own, sib = refs[0:4], refs[4:8]
    x_hbm, l_ref = refs[8:10]
    w_hbm, mix_ref, send_ref, gain_ref, sem, w_ref, x_ref = refs[10:]
    y = lax.axis_index("batch")
    s = lax.axis_index("seq")
    z, core = s // 2, s % 2
    x_copy = pltpu.make_async_copy(x_hbm, x_ref, sem.at[32])
    x_copy.start()
    copies = []
    for far in range(4):
        for near in range(4):
            first = ((y - far + 4) % 4) * 256 + ((z - near + 4) % 4) * 64
            for group, c in ((own, core), (sib, 1 - core)):
                row = pl.multiple_of(first + c * 32, 32)
                copies.append(
                    pltpu.make_async_copy(
                        group[far].at[near], w_ref.at[pl.ds(row, 32)], sem.at[len(copies)]
                    )
                )
    for copy in copies:
        copy.start()
    x_copy.wait()
    xs = x_ref[...]
    normed = xs * lax.rsqrt(jnp.mean(xs * xs, -1, keepdims=True) + EPS)
    for copy in copies:
        copy.wait()
    kept = [
        pltpu.make_async_copy(
            w_ref.at[pl.ds(i * 256, 256)], w_hbm.at[pl.ds(i * 256, 256)], sem.at[33 + i]
        )
        for i in range(4)
    ]
    for copy in kept:
        copy.start()
    last = w_ref[:, BETA:W1_COLS]
    row = lax.broadcasted_iota(jnp.int32, (8, 128), 0)
    lane = lax.broadcasted_iota(jnp.int32, (8, 128), 1)
    chosen = jnp.where(lane == row + 2, 1.0, 0.0).astype(bf16)
    gains = mm_nt(chosen, last)
    gain_ref[...] = gains
    mix = (normed * gains[0:1]).astype(bf16)
    mix_ref[...] = mix
    q = mm(mix, w_ref[:, 0:256]).astype(bf16)
    k = mm(mix, w_ref[:, 256:512]).astype(bf16)
    v = mm(mix, w_ref[:, 512:1024]).astype(bf16)
    logit = lax.dot_general(last, mix, (((0,), (1,)), ((), ())), preferred_element_type=f32)
    row16 = lax.broadcasted_iota(jnp.int32, (16, 128), 0)
    for j in range(8):
        seq, head, u = j // 4, (j // 2) % 2, j % 2
        rows = slice(seq * CHUNK, (seq + 1) * CHUNK)
        send_ref[j, 0:CHUNK, 0:128] = q[rows, head * 128 : (head + 1) * 128]
        send_ref[j, 0:CHUNK, 128:256] = k[rows, head * 128 : (head + 1) * 128]
        first = head * DV + u * HV
        send_ref[j, 0:CHUNK, 256:384] = v[rows, first : first + HV]
        b = logit[head : head + 1, rows]
        b_hi = b.astype(bf16).astype(f32)
        logs = l_ref[2 * seq + head : 2 * seq + head + 1, :]
        l_hi = logs.astype(bf16).astype(f32)
        l_mid = (logs - l_hi).astype(bf16).astype(f32)
        tile = jnp.zeros((16, 128), f32)
        for place, part in enumerate((b_hi, b - b_hi, l_hi, l_mid, (logs - l_hi) - l_mid)):
            tile = jnp.where(row16 == place, part, tile)
        send_ref[j, CHUNK:CHUNK_ROWS, 0:128] = tile.astype(bf16)
        send_ref[j, CHUNK:CHUNK_ROWS, 128:384] = jnp.zeros((16, 256), bf16)
    for copy in kept:
        copy.wait()


def gate_kernel(mix_ref, w_ref, gate_ref):
    gate_ref[...] = mm(mix_ref[...], w_ref[...])


def masks():
    i = lax.broadcasted_iota(jnp.int32, (CHUNK, CHUNK), 0)
    j = lax.broadcasted_iota(jnp.int32, (CHUNK, CHUNK), 1)
    return i, j


def inverses(systems, i, j):
    low = [n.astype(bf16) for n in systems]
    pair = (i >> 1) == (j >> 1)
    unit = jnp.where(i == j, 1.0, 0.0)
    out = [unit - jnp.where(pair, n, 0.0) for n in systems]
    zero = jnp.zeros((CHUNK, CHUNK), bf16)
    for level in range(1, 7):
        corner = ((i >> (level + 1)) == (j >> (level + 1))) & ((i >> level) != (j >> level))
        now = [v.astype(bf16) for v in out]
        half = [mm(now[c], jnp.where(corner, low[c], zero)).astype(bf16) for c in range(len(low))]
        out = [out[c] - mm(half[c], now[c]) for c in range(len(low))]
    now = [v.astype(bf16) for v in out]
    rest = []
    for c in range(len(low)):
        both = jnp.concatenate([low[c], (systems[c] - low[c].astype(f32)).astype(bf16)], 1)
        product = mm(both, jnp.concatenate([now[c], now[c]], 0))
        rest.append((unit - now[c].astype(f32) - product).astype(bf16))
    return [now[c].astype(f32) + mm(now[c], rest[c]) for c in range(len(low))]


def row_parts(recv_ref):
    tiles = [recv_ref[c, CHUNK:CHUNK_ROWS, 0:128].astype(f32) for c in range(NCHUNK)]
    betas = jnp.concatenate([t[0:1] + t[1:2] for t in tiles], 0)
    logs = jnp.concatenate([(t[2:3] + t[3:4]) + t[4:5] for t in tiles], 0)
    return sigmoid(betas.T), logs


def load_tokens(recv_ref, ext):
    ext[0:16, :] = jnp.zeros((16, CHAN), f32)
    for c in range(NCHUNK):
        ext[16 + c * CHUNK : 16 + (c + 1) * CHUNK, :] = recv_ref[c, 0:CHUNK, :].astype(f32)


def convolve(ext, taps, c):
    first = 16 + c * CHUNK - (KCONV - 1)
    pre = ext[pl.ds(first, CHUNK), :] * taps[0:1]
    for tap in range(1, KCONV):
        pre = pre + ext[pl.ds(first + tap, CHUNK), :] * taps[tap : tap + 1]
    return pre


def unit(a):
    scale = lax.rsqrt(jnp.sum(a * a, -1, keepdims=True) + EPS)
    return a * scale, scale


def spread_of(lrows, lcols, c, i, j):
    gap = lcols[:, c : c + 1] - lrows[c : c + 1, :]
    return jnp.where(i >= j, jnp.exp(jnp.where(i >= j, gap, 0.0)), 0.0)


def forward_kernel(
    recv_ref, taps_ref, mixed_ref, inv_ref, w_ref, u_ref, s_ref, q_ref, k_ref, p_ref, ext
):
    load_tokens(recv_ref, ext)
    taps = taps_ref[...]
    betas, lrows = row_parts(recv_ref)
    lcols = lrows.T
    i, j = masks()
    strict = i > j
    qs, ks, kds, ps, systems, rights, grown = [], [], [], [], [], [], []
    for c in range(NCHUNK):
        pre = convolve(ext, taps, c)
        act = pre * sigmoid(pre)
        q = unit(act[:, 0:128])[0].astype(bf16)
        k = unit(act[:, 128:256])[0].astype(bf16)
        v = act[:, 256:384].astype(bf16)
        q_ref[c] = q
        k_ref[c] = k
        spread = spread_of(lrows, lcols, c, i, j)
        beta = betas[:, c : c + 1]
        lcol = lcols[:, c : c + 1]
        ltop = lrows[c : c + 1, CHUNK - 1 : CHUNK]
        grow = jnp.exp(lcol)
        kf = k.astype(f32)
        systems.append(jnp.where(strict, beta * spread * mm_nt(k, k), 0.0))
        ps.append((spread * mm_nt(q, k)).astype(bf16))
        p_ref[c] = ps[c]
        rights.append(
            jnp.concatenate([beta * v.astype(f32), (beta * grow) * kf], 1).astype(bf16)
        )
        qs.append((grow * q.astype(f32)).astype(bf16))
        kds.append((jnp.exp(ltop - lcol) * kf).astype(bf16))
        grown.append(jnp.exp(ltop))
    inv = inverses(systems, i, j)
    us, ws = [], []
    for c in range(NCHUNK):
        low = inv[c].astype(bf16)
        inv_ref[c] = low
        both = mm(low, rights[c])
        us.append(both[:, 0:128])
        ws.append(both[:, 128:256].astype(bf16))
        w_ref[c] = ws[c]
    state = jnp.zeros((DK, HV), f32)
    for c in range(NCHUNK):
        start = state.astype(bf16)
        s_ref[c] = start
        u = (us[c] - mm(ws[c], start)).astype(bf16)
        u_ref[c] = u
        state = grown[c] * state + mm_tn(kds[c], u)
        mixed_ref[c] = (QF * (mm(qs[c], start) + mm(ps[c], u))).astype(bf16)


def backward_kernel(
    recv_ref, taps_ref, grad_ref, inv_ref, w_ref, u_ref, s_ref, q_ref, k_ref, p_ref,
    out_ref, tap_ref, ext, gext,
):
    load_tokens(recv_ref, ext)
    taps = taps_ref[...]
    betas, lrows = row_parts(recv_ref)
    lcols = lrows.T
    i, j = masks()
    strict = i > j
    gext[16 + NCHUNK * CHUNK :, :] = jnp.zeros((16, CHAN), f32)
    kept = []
    for c in range(NCHUNK):
        q, k = q_ref[c], k_ref[c]
        lcol = lcols[:, c : c + 1]
        ltop = lrows[c : c + 1, CHUNK - 1 : CHUNK]
        grow = jnp.exp(lcol)
        fade = jnp.exp(ltop - lcol)
        kd = (fade * k.astype(f32)).astype(bf16)
        grown_q = (QF * grow * q.astype(f32)).astype(bf16)
        g = grad_ref[c]
        du = QF * mm_tn(p_ref[c], g)
        ds = mm_tn(grown_q, g)
        kept.append((q, k, grow, fade, jnp.exp(ltop), kd, du, ds))
    state = jnp.zeros((DK, HV), f32)
    after, dus = [None] * NCHUNK, [None] * NCHUNK
    for c in reversed(range(NCHUNK)):
        top, kd, du, ds = kept[c][4:]
        low = state.astype(bf16)
        after[c] = low
        du = (du + mm(kd, low)).astype(bf16)
        dus[c] = du
        state = top * state + ds - mm_tn(w_ref[c], du)
    cols = []
    for c in range(NCHUNK):
        q, k, grow, fade = kept[c][:4]
        beta = betas[:, c : c + 1]
        spread = spread_of(lrows, lcols, c, i, j)
        g = grad_ref[c]
        u = u_ref[c]
        start = s_ref[c]
        pre = convolve(ext, taps, c)
        sig = sigmoid(pre)
        act = pre * sig
        v = act[:, 256:384].astype(bf16).astype(f32)
        dr = mm_tn(inv_ref[c], dus[c])
        drl = dr.astype(bf16)
        dp = (QF * spread * mm_nt(g, u)).astype(bf16)
        dt = jnp.where(strict, -spread * mm_nt(drl, u), 0.0)
        dkk = (beta * dt).astype(bf16)
        recalled = grow * mm(k, start)
        cols.append(
            jnp.sum(dt * mm_nt(k, k), -1, keepdims=True)
            + jnp.sum(dr * (v - recalled), -1, keepdims=True)
        )
        dq = mm(dp, k) + (QF * grow) * mm_nt(g, start)
        dk = (
            mm_tn(dp, q)
            + fade * mm_nt(u, after[c])
            + (mm(dkk, k) + mm_tn(dkk, k))
            - (beta * grow) * mm_nt(drl, start)
        )
        dv = beta * dr
        slope = sig * (1.0 + pre * (1.0 - sig))
        for first, part in ((0, dq), (128, dk)):
            a = act[:, first : first + 128]
            n, scale = unit(a)
            da = scale * (part - n * jnp.sum(n * part, -1, keepdims=True))
            gext[16 + c * CHUNK : 16 + (c + 1) * CHUNK, first : first + 128] = (
                da * slope[:, first : first + 128]
            )
        gext[16 + c * CHUNK : 16 + (c + 1) * CHUNK, 256:384] = dv * slope[:, 256:384]
    dbeta = jnp.concatenate(cols, 1) * betas * (1.0 - betas)
    brows = dbeta.T
    row16 = lax.broadcasted_iota(jnp.int32, (16, 128), 0)
    tap_sums = [jnp.zeros((1, CHAN), f32) for _ in range(KCONV)]
    for c in range(NCHUNK):
        here = 16 + c * CHUNK
        gpre = gext[here : here + CHUNK, :]
        total = gpre * taps[KCONV - 1 : KCONV]
        tap_sums[KCONV - 1] = tap_sums[KCONV - 1] + jnp.sum(
            gpre * ext[here : here + CHUNK, :], 0, keepdims=True
        )
        for tap in range(KCONV - 1):
            back = KCONV - 1 - tap
            total = total + gext[pl.ds(here + back, CHUNK), :] * taps[tap : tap + 1]
            tap_sums[tap] = tap_sums[tap] + jnp.sum(
                gpre * ext[pl.ds(here - back, CHUNK), :], 0, keepdims=True
            )
        out_ref[c, 0:CHUNK, :] = total.astype(bf16)
        b = brows[c : c + 1, :]
        hi = b.astype(bf16).astype(f32)
        tile = jnp.where(row16 == 0, hi, jnp.where(row16 == 1, b - hi, 0.0))
        out_ref[c, CHUNK:CHUNK_ROWS, 0:128] = tile.astype(bf16)
        out_ref[c, CHUNK:CHUNK_ROWS, 128:384] = jnp.zeros((16, 256), bf16)
    tap_ref[...] = jnp.concatenate(tap_sums + [jnp.zeros((8 - KCONV, CHAN), f32)], 0)


def head_parts(mixed_ref, gate_ref, gain, seq, head):
    a = mixed_ref[4 * seq + 2 * head].astype(f32)
    b = mixed_ref[4 * seq + 2 * head + 1].astype(f32)
    mean = (jnp.sum(a * a, -1, keepdims=True) + jnp.sum(b * b, -1, keepdims=True)) / DV
    scale = lax.rsqrt(mean + EPS)
    logit = gate_ref[seq * CHUNK : (seq + 1) * CHUNK, head * DV : (head + 1) * DV]
    n = jnp.concatenate([a, b], 1) * scale
    return n, scale, logit, sigmoid(logit), gain[:, head * DV : (head + 1) * DV]


def send_in_order(part_ref, outs):
    x = lax.axis_index("tensor")
    for d, out in enumerate(outs):
        out[...] = part_ref[pl.ds(pl.multiple_of(((x + d) % 4) * 64, 64), 64), :]


def output_kernel(
    mixed_ref, gate_ref, gain_ref, w_ref, gated_ref, o0, o1, o2, o3, part_ref
):
    gain = gain_ref[...].astype(f32)
    for seq in range(2):
        for head in range(2):
            n, _, logit, sig, own = head_parts(mixed_ref, gate_ref, gain, seq, head)
            gated_ref[seq * CHUNK : (seq + 1) * CHUNK, head * DV : (head + 1) * DV] = (
                n * own * (logit * sig)
            ).astype(bf16)
    part_ref[...] = mm_nt(gated_ref[...], w_ref[...]).astype(bf16)
    send_in_order(part_ref, (o0, o1, o2, o3))


def middle_kernel(o0, o1, o2, o3, x_ref, gain_ref, middle_ref, rows_ref):
    middle = x_ref[...] + added(o0, o1, o2, o3)
    middle_ref[...] = middle
    scale = lax.rsqrt(jnp.mean(middle * middle, -1, keepdims=True) + EPS)
    rows_ref[...] = (middle * scale * gain_ref[1:2, :]).astype(bf16)


def norm_back(g, v, gain):
    scale = lax.rsqrt(jnp.mean(v * v, -1, keepdims=True) + EPS)
    n = v * scale
    gg = g * gain
    return scale * (gg - n * jnp.mean(gg * n, -1, keepdims=True)), jnp.sum(g * n, 0, keepdims=True)


def added(o0, o1, o2, o3):
    return (o0[...].astype(f32) + o1[...].astype(f32)) + (o2[...].astype(f32) + o3[...].astype(f32))


def ffn_back_kernel(g0, g1, g2, g3, middle_ref, cot_ref, gain_ref, rows_ref, sum_ref):
    part, gain_sum = norm_back(added(g0, g1, g2, g3), middle_ref[...], gain_ref[1:2, :])
    grad = cot_ref[...].astype(f32) + part
    rows_ref[...] = grad.astype(bf16)
    sum_ref[...] = jnp.broadcast_to(gain_sum, sum_ref.shape)


def result_kernel(o0, o1, o2, o3, rows_ref):
    rows_ref[...] = added(o0, o1, o2, o3).astype(bf16)


def first_back_kernel(o0, o1, o2, o3, x_ref, grad_ref, gain_ref, out_ref):
    parts = [o[...].astype(f32) for o in (o1, o2, o3)]
    a, b, c = turned(parts, lax.axis_index("tensor"))
    part, _ = norm_back((o0[...].astype(f32) + a) + (b + c), x_ref[...], gain_ref[0:1, :])
    out_ref[...] = grad_ref[...].astype(f32) + part


def place_rows(blocks, out_ref):
    x = lax.axis_index("tensor")
    for d, block in enumerate(blocks):
        row = pl.multiple_of(((x - d + 4) % 4) * 64, 64)
        out_ref[pl.ds(row, 64), :] = block.astype(out_ref.dtype)


def place_kernel(c0, c1, c2, c3, out_ref):
    place_rows([c[...] for c in (c0, c1, c2, c3)], out_ref)


def output_back_kernel(
    c0, c1, c2, c3, mixed_ref, gate_ref, gain_ref, gated_ref, mix_ref, w_ref, gate_w_ref, given,
    gmix_ref, gmixed_ref, ggain_ref, part_ref, out_hbm, glogit_ref, sum_ref, sem,
):
    place_rows([c[...] for c in (c0, c1, c2, c3)], gmix_ref)
    gain = gain_ref[...].astype(f32)
    grad = mm(gmix_ref[...], w_ref[...])
    sums = []
    for head in range(2):
        total = jnp.zeros((1, DV), f32)
        for seq in range(2):
            n, scale, logit, sig, own = head_parts(mixed_ref, gate_ref, gain, seq, head)
            g = grad[seq * CHUNK : (seq + 1) * CHUNK, head * DV : (head + 1) * DV]
            t = g * (logit * sig)
            total = total + jnp.sum(t * n, 0, keepdims=True)
            gn = t * own
            gm = scale * (gn - n * jnp.mean(gn * n, -1, keepdims=True))
            gmixed_ref[4 * seq + 2 * head] = gm[:, 0:128].astype(bf16)
            gmixed_ref[4 * seq + 2 * head + 1] = gm[:, 128:256].astype(bf16)
            slope = sig * (1.0 + logit * (1.0 - sig))
            glogit_ref[seq * CHUNK : (seq + 1) * CHUNK, head * DV : (head + 1) * DV] = (
                g * n * own * slope
            ).astype(bf16)
        sums.append(total)
    ggain_ref[...] = jnp.broadcast_to(jnp.concatenate(sums, 1), (8, 2 * DV))
    copies = []
    for i, (left, right) in enumerate(((gmix_ref, gated_ref), (mix_ref, glogit_ref))):
        sum_ref[i] = mm_tn(left[...], right[...]).astype(bf16)
        copies.append(
            pltpu.make_async_copy(sum_ref.at[i], out_hbm.at[:, pl.ds(i * 512, 512)], sem.at[i])
        )
        copies[i].start()
    part_ref[...] = mm_nt(glogit_ref[...], gate_w_ref[...])
    for copy in copies:
        copy.wait()


def ffn_kernel(
    r0, r1, r2, r3, cot_hbm, w_hbm, middle_ref, g0, g1, g2, g3, p0, p1, p2, p3,
    hidden_ref, ggate_ref, gup_ref, in_ref, cot_ref, w_ref, sem,
):
    rows = [
        pltpu.make_async_copy(ref, in_ref.at[pl.ds(d * 64, 64)], sem.at[d])
        for d, ref in enumerate((r0, r1, r2, r3))
    ]
    weights = [
        [
            pltpu.make_async_copy(
                w_hbm.at[pl.ds(r * 256, 256), pl.ds(FFN + i * FFP, FFP)],
                w_ref.at[i, pl.ds(r * 256, 256)],
                sem.at[5 + 4 * i + r],
            )
            for r in range(4)
        ]
        for i in range(3)
    ]
    cot_copy = pltpu.make_async_copy(cot_hbm, cot_ref, sem.at[4])
    for copy in rows + weights[0] + weights[1] + [cot_copy] + weights[2]:
        copy.start()
    for copy in rows + weights[0]:
        copy.wait()
    tokens = in_ref[...]
    gate = mm(tokens, w_ref[0])
    for copy in weights[1]:
        copy.wait()
    up = mm(tokens, w_ref[1])
    for copy in [cot_copy] + weights[2]:
        copy.wait()
    ghidden = mm(cot_ref[...], w_ref[2])
    sig = sigmoid(gate)
    silu = gate * sig
    ggate = (ghidden * up * (sig * (1.0 + gate * (1.0 - sig)))).astype(bf16)
    gup = (ghidden * silu).astype(bf16)
    hidden = (silu * up).astype(bf16)
    hidden_ref[...] = hidden
    ggate_ref[...] = ggate
    gup_ref[...] = gup
    gpart = (mm_nt(ggate, w_ref[0]) + mm_nt(gup, w_ref[1])).astype(bf16)
    part = mm_nt(hidden, w_ref[2])
    for d in range(4):
        (g0, g1, g2, g3)[d][...] = gpart[d * 64 : (d + 1) * 64]
        own = part[d * 64 : (d + 1) * 64]
        if d == 0:
            own = own + middle_ref[...]
        (p0, p1, p2, p3)[d][...] = own.astype(bf16)


def ffn_weight_kernel(
    r0, r1, r2, r3, cot_ref, hidden_ref, ggate_ref, gup_ref, out_hbm, in_ref, part_ref, sem
):
    for d, ref in enumerate((r0, r1, r2, r3)):
        in_ref[d * 64 : (d + 1) * 64, :] = ref[...]
    copies = []
    for i, (left, right) in enumerate(
        ((in_ref, ggate_ref), (in_ref, gup_ref), (cot_ref, hidden_ref))
    ):
        part_ref[i] = mm_tn(left[...], right[...]).astype(bf16)
        copies.append(
            pltpu.make_async_copy(
                part_ref.at[i], out_hbm.at[:, pl.ds(FFN + i * FFP, FFP)], sem.at[i]
            )
        )
        copies[i].start()
    for copy in copies:
        copy.wait()


def second_split_kernel(in_ref, out_ref, gate_ref, a_ref, b_ref, c_ref):
    out_ref[...] = in_ref[:, 0:512].astype(f32)
    gate_ref[...] = in_ref[:, 512:1024].astype(f32)
    for i, ref in enumerate((a_ref, b_ref, c_ref)):
        ref[...] = in_ref[:, FFN + i * FFP : FFN + i * FFP + FF].astype(f32)


def core_split(value, core, mine_ref, other_ref, y):
    value = value.reshape(4, 2, 32, value.shape[-1])
    first, second = value[:, 0], value[:, 1]
    mine = jnp.where(core == 0, first, second)
    other = jnp.where(core == 0, second, first)
    rows = slice(y * 128, (y + 1) * 128)
    mine_ref[rows, :] = mine.reshape(128, W1_COLS)
    other_ref[rows, :] = other.reshape(128, W1_COLS)


def coded(small):
    hi = small.astype(bf16).astype(f32)
    lo = (small - hi).astype(bf16).astype(f32)
    tile = jnp.concatenate([hi, lo], 0)
    tile = jnp.concatenate([tile, jnp.zeros((16, W1_COLS - 1024), f32)], 1)
    return tile.astype(bf16), hi + lo


def decoded(tile):
    tile = tile[:, 0:1024].astype(f32)
    return tile[0:8] + tile[8:16]


def project_back_kernel(
    recv_ref,
    mix_ref,
    gate_part_ref,
    w_ref,
    x_ref,
    taps_ref,
    ggain_ref,
    fgain_ref,
    part_ref,
    mine_ref,
    other_ref,
    small_ref,
    dproj_ref,
    row_ref,
):
    s = lax.axis_index("seq")
    core, head_here = s % 2, (s // 2) % 2
    row = lax.broadcasted_iota(jnp.int32, (128, 128), 0)
    for seq in range(2):
        rows = slice(seq * CHUNK, (seq + 1) * CHUNK)
        beta = jnp.zeros((128, 128), f32)
        for head in range(2):
            ja = 4 * seq + 2 * head
            a, b = recv_ref.at[ja], recv_ref.at[ja + 1]
            for first in (0, 128):
                total = a[0:CHUNK, first : first + 128].astype(f32) + b[
                    0:CHUNK, first : first + 128
                ].astype(f32)
                place = 2 * first + head * 128
                dproj_ref[rows, place : place + 128] = total.astype(bf16)
            dproj_ref[rows, 512 + head * 256 : 640 + head * 256] = a[0:CHUNK, 256:384]
            dproj_ref[rows, 640 + head * 256 : 768 + head * 256] = b[0:CHUNK, 256:384]
            both = a[CHUNK:CHUNK_ROWS, 0:128].astype(f32) + b[CHUNK:CHUNK_ROWS, 0:128].astype(f32)
            beta = jnp.where(row == head, both[0:1] + both[1:2], beta)
        dproj_ref[rows, BETA:W1_COLS] = beta.T.astype(bf16)
    part = mm_nt(dproj_ref[...], w_ref[...]) + gate_part_ref[...]
    part_ref[...] = part.astype(bf16)
    xs = x_ref[...]
    mix_sum = jnp.sum(
        part * (xs * lax.rsqrt(jnp.mean(xs * xs, -1, keepdims=True) + EPS)), 0, keepdims=True
    )
    row_ref[...] = jnp.zeros((8, 1024), f32)
    for first, base in (
        (0, head_here * 128),
        (128, 256 + head_here * 128),
        (256, 512 + head_here * 256 + core * 128),
    ):
        lanes = pl.ds(pl.multiple_of(base, 128), 128)
        row_ref[0:8, lanes] = taps_ref[0:8, first : first + 128]
    row_ref[4:5, 0:512] = ggain_ref[0:1, :]
    row_ref[5:6, :] = mix_sum
    row_ref[6:7, :] = fgain_ref[0:1, :]
    tile, value = coded(row_ref[...])
    small_ref[...] = value
    other_ref[512:528, :] = tile
    for y in range(4):
        value = mm_tn(mix_ref[:, y * 256 : (y + 1) * 256], dproj_ref[...]).astype(bf16)
        core_split(value, core, mine_ref, other_ref, y)


def turned(got, index):
    even = index % 2 == 0
    return jnp.where(even, got[2], got[0]), got[1], jnp.where(even, got[0], got[2])


def fold_kernel(axis, base_ref, *refs):
    count = 1 if axis == "batch" else 3
    got, small_ref, outs, small_out = refs[:count], refs[count], refs[count + 1 : -1], refs[-1]
    y, z = lax.axis_index("batch"), lax.axis_index("seq") // 2
    here = y if axis == "batch" else z
    size = outs[0].shape[0]
    parts = [decoded(g[4 * size : 4 * size + 16, :]) for g in got]
    if count == 1:
        small = small_ref[...] + parts[0]
    else:
        a, b, c = turned(parts, y)
        small = (small_ref[...] + a) + (b + c)
    tile, value = coded(small)
    small_out[...] = value
    for d, out in enumerate(outs):
        rows = pl.ds(pl.multiple_of(((here + d) % 4) * size, 32), size)
        total = base_ref[rows, :].astype(f32)
        for g in got:
            total = total + g[rows, :].astype(f32)
        out[0:size, :] = total.astype(out.dtype)
        if d > 0:
            out[size : size + 16, :] = tile


def first_out_kernel(
    base_ref, g1, g2, g3, small_ref,
    q_ref, k_ref, v_ref, beta_ref, tap_q_ref, tap_k_ref, tap_v_ref, out_gain_ref, gain_ref,
):
    got = (g1, g2, g3)
    total = base_ref[...]
    for g in got:
        total = total + g[0:32, :].astype(f32)
    q_ref[...] = total[:, 0:256]
    k_ref[...] = total[:, 256:512]
    v_ref[...] = total[:, 512:1024]
    beta_ref[...] = total[:, BETA:W1_COLS].T[0:2, :]
    a, b, c = turned([decoded(g[32:48, :]) for g in got], lax.axis_index("seq") // 2)
    small = (small_ref[...] + a) + (b + c)
    tap_q_ref[...] = small[0:4, 0:256]
    tap_k_ref[...] = small[0:4, 256:512]
    tap_v_ref[...] = small[0:4, 512:1024]
    out_gain_ref[...] = small[4:5, 0:512]
    place = (lax.axis_index("batch") * 8 + lax.axis_index("seq")) * 32
    gain_ref[...] = pltpu.roll(small, (1024 - place) % 1024, 1)[:, 0:128]


def gain_kernel(g0, g1, g2, g3, mix_ref, ffn_ref):
    a, b, c = turned([g1[...], g2[...], g3[...]], lax.axis_index("tensor"))
    total = (g0[...] + a) + (b + c)
    mix_ref[...] = total[5:6, 0:32]
    ffn_ref[...] = total[6:7, 0:32]


vmem = pl.BlockSpec(memory_space=pltpu.VMEM)
hbm = pl.BlockSpec(memory_space=pl.ANY)


def call(kernel, outs, *args, scratch=(), in_specs=None, out_specs=None, windowed=False, alias=None, name=None, mb=8):
    grid = {"grid": (1,)} if windowed else {}
    return pl.pallas_call(
        kernel,
        **grid,
        out_shape=[jax.ShapeDtypeStruct(shape, dtype) for shape, dtype in outs],
        in_specs=in_specs or [vmem] * len(args),
        out_specs=out_specs or [vmem] * len(outs),
        input_output_aliases=alias or {},
        scratch_shapes=list(scratch),
        compiler_params=pltpu.CompilerParams(vmem_limit_bytes=mb * 1024 * 1024),
        cost_estimate=pl.CostEstimate(flops=COST, bytes_accessed=COST, transcendentals=0),
        name=name,
    )(*args)


def fold(axis, base, got, small, size, name):
    outs = [((size, W1_COLS), f32)] + [((size + 16, W1_COLS), bf16)] * 3 + [((8, 1024), f32)]
    *out, small = call(partial(fold_kernel, axis), outs, base, *got, small, name=name, mb=12)
    return out, small


def per_device(
    inputs,
    decay_rate,
    cotangent,
    mix_gain,
    query_weight,
    key_weight,
    value_weight,
    gate_weight,
    beta_weight,
    conv_query,
    conv_key,
    conv_value,
    out_gain,
    output_weight,
    ffn_gain,
    ffn_gate,
    ffn_up,
    ffn_down,
):
    s = lax.axis_index("seq")
    x = lax.axis_index("tensor")
    head, half = (s // 2) % 2, s % 2
    tokens = inputs.reshape(256, 1024)
    cot = cotangent.reshape(256, 1024)

    logs = jnp.cumsum(jnp.log(decay_rate), 1).transpose(0, 2, 1).reshape(4, CHUNK)
    logs = jnp.pad(logs, ((0, 4), (0, 0)))
    (shard1,) = call(
        first_pack_kernel,
        [((32, W1_COLS), bf16)],
        query_weight,
        key_weight,
        value_weight,
        beta_weight.T,
        mix_gain[None],
        ffn_gain[None],
        name="first_pack",
        mb=56,
    )
    column = jnp.stack([shard1] + [move_z(shard1, d) for d in (1, 2, 3)])

    output_weight, column, logs = lax.optimization_barrier((output_weight, column, logs))
    (shard2,) = call(
        second_pack_kernel,
        [((32, W2_COLS), bf16)],
        output_weight,
        gate_weight,
        ffn_gate,
        ffn_up,
        ffn_down,
        name="second_pack",
        mb=56,
    )
    own = [column] + [move_y(column, d) for d in (1, 2, 3)]
    sib = [move_core(v) for v in own]
    w2 = lax.all_gather(shard2, ("batch", "seq"), axis=0, tiled=True)

    taps = jnp.concatenate(
        [
            lax.dynamic_slice_in_dim(conv_query.T, head * DK, DK, 1),
            lax.dynamic_slice_in_dim(conv_key.T, head * DK, DK, 1),
            lax.dynamic_slice_in_dim(conv_value.T, head * DV + half * HV, HV, 1),
        ],
        1,
    ).astype(f32)
    taps = jnp.pad(taps, ((0, 8 - KCONV), (0, 0)))
    gain_row = out_gain[None]
    own_tokens = pick(tokens.reshape(4, 64, 1024), x)
    cot4 = cot.reshape(4, 64, 1024)
    own_cot = pick(cot4, x)
    cot_turned = jnp.concatenate([pick(cot4, (x - d) % 4) for d in range(4)], 0)

    w1, mix_input, send, gains = call(
        project_kernel,
        [
            ((1024, W1_COLS), bf16),
            ((256, 1024), bf16),
            ((8, CHUNK_ROWS, CHAN), bf16),
            ((8, 1024), f32),
        ],
        *own,
        *sib,
        tokens,
        logs,
        scratch=[
            pltpu.SemaphoreType.DMA((37,)),
            pltpu.VMEM((1024, W1_COLS), bf16),
            pltpu.VMEM((256, 1024), f32),
        ],
        in_specs=[hbm] * 9 + [vmem],
        out_specs=[hbm] + [vmem] * 3,
        name="project",
        mb=56,
    )
    recv = lax.all_to_all(send, "seq", 0, 0)
    square = ((NCHUNK, 128, 128), bf16)
    mixed, *saved = call(
        forward_kernel,
        [square] * 8,
        recv,
        taps,
        scratch=[pltpu.VMEM((16 + NCHUNK * CHUNK, CHAN), f32)],
        name="delta_forward",
        mb=56,
    )
    mixed = lax.all_to_all(mixed, "seq", 0, 0)
    out_w = pl.BlockSpec((1024, 512), lambda i: (0, 0))
    gate_w = pl.BlockSpec((1024, 512), lambda i: (0, 1))
    (gate_logit,) = call(
        gate_kernel,
        [((256, 512), f32)],
        mix_input,
        w2,
        in_specs=[vmem, gate_w],
        windowed=True,
        name="gate",
        mb=56,
    )
    quarter = ((64, 1024), bf16)
    gated, *pieces = call(
        output_kernel,
        [((256, 512), bf16)] + [quarter] * 4,
        mixed,
        gate_logit,
        gain_row,
        w2,
        in_specs=[vmem] * 3 + [out_w],
        scratch=[pltpu.VMEM((256, 1024), bf16)],
        windowed=True,
        name="output",
        mb=56,
    )
    middle, ffn_rows = call(
        middle_kernel,
        [((64, 1024), f32), quarter],
        pieces[0],
        *[move_x(pieces[d], d) for d in (1, 2, 3)],
        own_tokens,
        gains,
        name="middle",
        mb=56,
    )
    ffn_blocks = gather_x(ffn_rows)
    hidden_shape = ((256, FFP), bf16)
    ffn_out = call(
        ffn_kernel,
        [quarter] * 8 + [hidden_shape] * 3,
        *ffn_blocks,
        cot_turned,
        w2,
        middle,
        in_specs=[hbm] * 6 + [vmem],
        scratch=[
            pltpu.VMEM((256, 1024), bf16),
            pltpu.VMEM((256, 1024), bf16),
            pltpu.VMEM((3, 1024, FFP), bf16),
            pltpu.SemaphoreType.DMA((17,)),
        ],
        name="ffn",
        mb=56,
    )
    gpieces, rpieces, (hidden, ggate, gup) = ffn_out[:4], tuple(ffn_out[4:8]), ffn_out[8:]
    got = [move_x(gpieces[d], -d) for d in (1, 2, 3)]
    (grad_w2,) = call(
        ffn_weight_kernel,
        [((1024, W2_COLS), bf16)],
        *ffn_blocks,
        cot_turned,
        hidden,
        ggate,
        gup,
        out_specs=[hbm],
        scratch=[
            pltpu.VMEM((256, 1024), bf16),
            pltpu.VMEM((3, 1024, FFP), bf16),
            pltpu.SemaphoreType.DMA((3,)),
        ],
        name="ffn_weight",
        mb=56,
    )
    middle, grad_w2 = lax.optimization_barrier((middle, grad_w2))
    grad_rows, ffn_gain_sum = call(
        ffn_back_kernel,
        [quarter, ((8, 1024), f32)],
        gpieces[0],
        *got,
        middle,
        own_cot,
        gains,
        name="ffn_back",
        mb=56,
    )
    mix_blocks = gather_x(grad_rows)
    grad_mix, gmixed, ggain, gate_part, grad_w2 = call(
        output_back_kernel,
        [
            ((256, 1024), bf16),
            ((8, CHUNK, 128), bf16),
            ((8, 512), f32),
            ((256, 1024), f32),
            ((1024, W2_COLS), bf16),
        ],
        *mix_blocks,
        mixed,
        gate_logit,
        gain_row,
        gated,
        mix_input,
        w2,
        w2,
        grad_w2,
        in_specs=[vmem] * 9 + [out_w, gate_w, hbm],
        out_specs=[vmem] * 4 + [hbm],
        scratch=[
            pltpu.VMEM((256, 512), bf16),
            pltpu.VMEM((2, 1024, 512), bf16),
            pltpu.SemaphoreType.DMA((2,)),
        ],
        windowed=True,
        alias={11: 4},
        name="output_back",
        mb=56,
    )
    rpieces, gmixed = lax.optimization_barrier((rpieces, gmixed))
    rgot = tuple(move_x(rpieces[d], -d) for d in (1, 2, 3))
    gmixed = lax.all_to_all(gmixed, "seq", 0, 0)
    grad_w2 = lax.psum_scatter(grad_w2, ("batch", "seq"), scatter_dimension=0, tiled=True)
    gsend, gtaps = call(
        backward_kernel,
        [((8, CHUNK_ROWS, CHAN), bf16), ((8, CHAN), f32)],
        recv,
        taps,
        gmixed,
        *saved,
        scratch=[
            pltpu.VMEM((16 + NCHUNK * CHUNK, CHAN), f32),
            pltpu.VMEM((32 + NCHUNK * CHUNK, CHAN), f32),
        ],
        name="delta_backward",
        mb=56,
    )
    gsend, rgot = lax.optimization_barrier((gsend, rgot))
    grecv = lax.all_to_all(gsend, "seq", 0, 0)
    (result_rows,) = call(
        result_kernel,
        [quarter],
        rpieces[0],
        *rgot,
        name="result_rows",
        mb=56,
    )
    result_blocks = gather_x(result_rows)
    grecv, result_blocks = lax.optimization_barrier((grecv, result_blocks))
    part, mine, other, small = call(
        project_back_kernel,
        [
            ((256, 1024), bf16),
            ((512, W1_COLS), bf16),
            ((528, W1_COLS), bf16),
            ((8, 1024), f32),
        ],
        grecv,
        mix_input,
        gate_part,
        w1,
        tokens,
        gtaps,
        ggain,
        ffn_gain_sum,
        scratch=[
            pltpu.VMEM((256, W1_COLS), bf16),
            pltpu.VMEM((8, 1024), f32),
        ],
        name="project_back",
        mb=28,
    )
    out, small = fold("batch", mine, [move_core(other)], small, 128, "first_core")
    got = [move_y(out[d], d) for d in (1, 2, 3)]
    part_2 = move_x(part, 2)
    (result,) = call(place_kernel, [((256, 1024), f32)], *result_blocks, name="result")
    got, result = lax.optimization_barrier((got, result))
    out, small = fold("seq", out[0], got, small, 32, "first_y")
    out, part = lax.optimization_barrier((out, part))
    got = [move_z(out[d], d) for d in (1, 2, 3)]
    (grad_inputs,) = call(
        first_back_kernel,
        [((256, 1024), f32)],
        part,
        move_x(part, 1),
        part_2,
        move_x(part, 3),
        tokens,
        grad_mix,
        gains,
        name="first_back",
        mb=14,
    )
    grad_q, grad_k, grad_v, grad_beta, tap_q, tap_k, tap_v, grad_out_gain, gain_rows = call(
        first_out_kernel,
        [
            ((32, 256), f32),
            ((32, 256), f32),
            ((32, 512), f32),
            ((2, 32), f32),
            ((4, 256), f32),
            ((4, 256), f32),
            ((4, 512), f32),
            ((1, 512), f32),
            ((8, 128), f32),
        ],
        out[0],
        *got,
        small,
        name="first_z",
    )
    grad_out_w, grad_gate_w, grad_fgate, grad_fup, grad_fdown = call(
        second_split_kernel,
        [((32, 512), f32)] * 2 + [((32, FF), f32)] * 3,
        grad_w2,
        name="second_split",
        mb=10,
    )
    grad_mix_gain, grad_ffn_gain = call(
        gain_kernel, [((1, 32), f32)] * 2, *gather_x(gain_rows), name="gain_sums"
    )
    return (
        result.reshape(2, 128, 1024),
        grad_inputs.reshape(2, 128, 1024),
        grad_mix_gain[0],
        grad_q,
        grad_k,
        grad_v,
        grad_gate_w,
        grad_beta.T,
        tap_q.T,
        tap_k.T,
        tap_v.T,
        grad_out_gain[0],
        grad_out_w,
        grad_ffn_gain[0],
        grad_fgate,
        grad_fup,
        grad_fdown,
    )


def solution(mesh):
    rows = ("batch", "seq")
    split = P(rows, "tensor")
    tokens = P("batch", "seq", None)
    taps = P("tensor", None)
    placed = (
        tokens,
        P("batch", "seq", "tensor"),
        tokens,
        P(rows),
        split,
        split,
        split,
        split,
        split,
        taps,
        taps,
        taps,
        P("tensor"),
        split,
        P(rows),
        split,
        split,
        split,
    )
    return jax.shard_map(
        per_device,
        mesh=mesh,
        in_specs=placed,
        out_specs=(
            tokens,
            tokens,
            P(rows),
            split,
            split,
            split,
            split,
            split,
            taps,
            taps,
            taps,
            P("tensor"),
            split,
            P(rows),
            split,
            split,
            split,
        ),
        check_vma=False,
    )
```

```python
from functools import partial

import jax
import jax.numpy as jnp
from jax import lax
from jax.experimental import pallas as pl
from jax.experimental.pallas import tpu as pltpu
from jax.sharding import PartitionSpec as P

bf16 = jnp.bfloat16
f32 = jnp.float32

DK = 128
DV = 256
HV = 128
KCONV = 4
CHUNK = 128
NCHUNK = 8
CHUNK_ROWS = CHUNK + 16
CHAN = 2 * DK + HV
W1_COLS = 1152
FF = 704
FFP = 768
FFN = 1024
W2_COLS = FFN + 3 * FFP
BETA = 1024
EPS = 1e-06
QF = DK ** (-0.5)
COST = 1000


def move_core(v):
    return lax.ppermute(v, "seq", [(i, i ^ 1) for i in range(8)])


def move_z(v, d):
    return lax.ppermute(v, "seq", [(i, (i + 2 * d) % 8) for i in range(8)])


def move_y(v, d):
    return lax.ppermute(v, "batch", [(i, (i + d) % 4) for i in range(4)])


def move_x(v, d):
    return lax.ppermute(v, "tensor", [(i, (i + d) % 4) for i in range(4)])


def pick(v, i):
    return lax.dynamic_index_in_dim(v, i, 0, keepdims=False)


def gather_x(rows):
    return [rows] + [move_x(rows, d) for d in (1, 2, 3)]


def mm(a, b):
    return jnp.dot(a.astype(bf16), b.astype(bf16), preferred_element_type=f32)


def mm_nt(a, b):
    return lax.dot_general(
        a.astype(bf16), b.astype(bf16), (((1,), (1,)), ((), ())), preferred_element_type=f32
    )


def mm_tn(a, b):
    return lax.dot_general(
        a.astype(bf16), b.astype(bf16), (((0,), (0,)), ((), ())), preferred_element_type=f32
    )


def sigmoid(v):
    return 1.0 / (1.0 + jnp.exp(-v))


def first_pack_kernel(q_ref, k_ref, v_ref, beta_ref, mix_ref, ffn_ref, out_ref):
    out_ref[:, 0:256] = q_ref[...]
    out_ref[:, 256:512] = k_ref[...]
    out_ref[:, 512:1024] = v_ref[...]
    row = lax.broadcasted_iota(jnp.int32, (128, 32), 0)
    last = jnp.zeros((128, 32), f32)
    beta = beta_ref[...].astype(f32)
    for place, part in enumerate(
        (beta[0:1], beta[1:2], mix_ref[...].astype(f32), ffn_ref[...].astype(f32))
    ):
        last = jnp.where(row == place, part, last)
    out_ref[:, BETA:W1_COLS] = last.T.astype(bf16)


def second_pack_kernel(out_w_ref, gate_ref, fgate_ref, fup_ref, fdown_ref, out_ref):
    out_ref[:, 0:512] = out_w_ref[...]
    out_ref[:, 512:1024] = gate_ref[...]
    for place, ref in enumerate((fgate_ref, fup_ref, fdown_ref)):
        first = FFN + place * FFP
        out_ref[:, first + 640 : first + FFP] = jnp.zeros((32, 128), bf16)
        out_ref[:, first : first + FF] = ref[...]


def project_kernel(*refs):
    own, sib = refs[0:4], refs[4:8]
    x_hbm, l_hbm = refs[8:10]
    w_hbm, mix_ref, send_ref, gain_ref, sem, w_ref, x_ref, l_ref = refs[10:]
    y = lax.axis_index("batch")
    s = lax.axis_index("seq")
    z, core = s // 2, s % 2
    x_copy = pltpu.make_async_copy(x_hbm, x_ref, sem.at[32])
    x_copy.start()
    l_copy = pltpu.make_async_copy(l_hbm, l_ref, sem.at[37])
    l_copy.start()
    copies = []
    for far in range(4):
        for near in range(4):
            first = ((y - far + 4) % 4) * 256 + ((z - near + 4) % 4) * 64
            for group, c in ((own, core), (sib, 1 - core)):
                row = pl.multiple_of(first + c * 32, 32)
                copies.append(
                    pltpu.make_async_copy(
                        group[far].at[near], w_ref.at[pl.ds(row, 32)], sem.at[len(copies)]
                    )
                )
    for copy in copies:
        copy.start()
    x_copy.wait()
    l_copy.wait()
    xs = x_ref[...]
    normed = xs * lax.rsqrt(jnp.mean(xs * xs, -1, keepdims=True) + EPS)
    for copy in copies:
        copy.wait()
    kept = [
        pltpu.make_async_copy(
            w_ref.at[pl.ds(i * 256, 256)], w_hbm.at[pl.ds(i * 256, 256)], sem.at[33 + i]
        )
        for i in range(4)
    ]
    for copy in kept:
        copy.start()
    last = w_ref[:, BETA:W1_COLS]
    row = lax.broadcasted_iota(jnp.int32, (8, 128), 0)
    lane = lax.broadcasted_iota(jnp.int32, (8, 128), 1)
    chosen = jnp.where(lane == row + 2, 1.0, 0.0).astype(bf16)
    gains = mm_nt(chosen, last)
    gain_ref[...] = gains
    mix = (normed * gains[0:1]).astype(bf16)
    mix_ref[...] = mix
    q = mm(mix, w_ref[:, 0:256]).astype(bf16)
    k = mm(mix, w_ref[:, 256:512]).astype(bf16)
    v = mm(mix, w_ref[:, 512:1024]).astype(bf16)
    logit = lax.dot_general(last, mix, (((0,), (1,)), ((), ())), preferred_element_type=f32)
    row16 = lax.broadcasted_iota(jnp.int32, (16, 128), 0)
    for j in range(8):
        seq, head, u = j // 4, (j // 2) % 2, j % 2
        rows = slice(seq * CHUNK, (seq + 1) * CHUNK)
        send_ref[j, 0:CHUNK, 0:128] = q[rows, head * 128 : (head + 1) * 128]
        send_ref[j, 0:CHUNK, 128:256] = k[rows, head * 128 : (head + 1) * 128]
        first = head * DV + u * HV
        send_ref[j, 0:CHUNK, 256:384] = v[rows, first : first + HV]
        b = logit[head : head + 1, rows]
        b_hi = b.astype(bf16).astype(f32)
        logs = l_ref[2 * seq + head : 2 * seq + head + 1, :]
        l_hi = logs.astype(bf16).astype(f32)
        l_mid = (logs - l_hi).astype(bf16).astype(f32)
        tile = jnp.zeros((16, 128), f32)
        for place, part in enumerate((b_hi, b - b_hi, l_hi, l_mid, (logs - l_hi) - l_mid)):
            tile = jnp.where(row16 == place, part, tile)
        send_ref[j, CHUNK:CHUNK_ROWS, 0:128] = tile.astype(bf16)
        send_ref[j, CHUNK:CHUNK_ROWS, 128:384] = jnp.zeros((16, 256), bf16)
    for copy in kept:
        copy.wait()


def gate_kernel(mix_ref, w_ref, gate_ref):
    gate_ref[...] = mm(mix_ref[...], w_ref[...])


def masks():
    i = lax.broadcasted_iota(jnp.int32, (CHUNK, CHUNK), 0)
    j = lax.broadcasted_iota(jnp.int32, (CHUNK, CHUNK), 1)
    return i, j


def inverses(systems, i, j):
    low = [n.astype(bf16) for n in systems]
    pair = (i >> 1) == (j >> 1)
    unit = jnp.where(i == j, 1.0, 0.0)
    out = [unit - jnp.where(pair, n, 0.0) for n in systems]
    zero = jnp.zeros((CHUNK, CHUNK), bf16)
    for level in range(1, 7):
        corner = ((i >> (level + 1)) == (j >> (level + 1))) & ((i >> level) != (j >> level))
        now = [v.astype(bf16) for v in out]
        half = [mm(now[c], jnp.where(corner, low[c], zero)).astype(bf16) for c in range(len(low))]
        out = [out[c] - mm(half[c], now[c]) for c in range(len(low))]
    now = [v.astype(bf16) for v in out]
    rest = []
    for c in range(len(low)):
        both = jnp.concatenate([low[c], (systems[c] - low[c].astype(f32)).astype(bf16)], 1)
        product = mm(both, jnp.concatenate([now[c], now[c]], 0))
        rest.append((unit - now[c].astype(f32) - product).astype(bf16))
    return [now[c].astype(f32) + mm(now[c], rest[c]) for c in range(len(low))]


def row_parts(recv_ref):
    tiles = [recv_ref[c, CHUNK:CHUNK_ROWS, 0:128].astype(f32) for c in range(NCHUNK)]
    betas = jnp.concatenate([t[0:1] + t[1:2] for t in tiles], 0)
    logs = jnp.concatenate([(t[2:3] + t[3:4]) + t[4:5] for t in tiles], 0)
    return sigmoid(betas.T), logs


def load_tokens(recv_ref, ext):
    ext[0:16, :] = jnp.zeros((16, CHAN), f32)
    for c in range(NCHUNK):
        ext[16 + c * CHUNK : 16 + (c + 1) * CHUNK, :] = recv_ref[c, 0:CHUNK, :].astype(f32)


def convolve(ext, taps, c):
    first = 16 + c * CHUNK - (KCONV - 1)
    pre = ext[pl.ds(first, CHUNK), :] * taps[0:1]
    for tap in range(1, KCONV):
        pre = pre + ext[pl.ds(first + tap, CHUNK), :] * taps[tap : tap + 1]
    return pre


def unit(a):
    scale = lax.rsqrt(jnp.sum(a * a, -1, keepdims=True) + EPS)
    return a * scale, scale


def spread_of(lrows, lcols, c, i, j):
    gap = lcols[:, c : c + 1] - lrows[c : c + 1, :]
    return jnp.where(i >= j, jnp.exp(jnp.where(i >= j, gap, 0.0)), 0.0)


def forward_kernel(
    recv_ref, taps_ref, mixed_ref, inv_ref, w_ref, u_ref, s_ref, q_ref, k_ref, p_ref, ext
):
    load_tokens(recv_ref, ext)
    taps = taps_ref[...]
    betas, lrows = row_parts(recv_ref)
    lcols = lrows.T
    i, j = masks()
    strict = i > j
    qs, ks, kds, ps, systems, rights, grown = [], [], [], [], [], [], []
    for c in range(NCHUNK):
        pre = convolve(ext, taps, c)
        act = pre * sigmoid(pre)
        q = unit(act[:, 0:128])[0].astype(bf16)
        k = unit(act[:, 128:256])[0].astype(bf16)
        v = act[:, 256:384].astype(bf16)
        q_ref[c] = q
        k_ref[c] = k
        spread = spread_of(lrows, lcols, c, i, j)
        beta = betas[:, c : c + 1]
        lcol = lcols[:, c : c + 1]
        ltop = lrows[c : c + 1, CHUNK - 1 : CHUNK]
        grow = jnp.exp(lcol)
        kf = k.astype(f32)
        systems.append(jnp.where(strict, beta * spread * mm_nt(k, k), 0.0))
        ps.append((spread * mm_nt(q, k)).astype(bf16))
        p_ref[c] = ps[c]
        rights.append(
            jnp.concatenate([beta * v.astype(f32), (beta * grow) * kf], 1).astype(bf16)
        )
        qs.append((grow * q.astype(f32)).astype(bf16))
        kds.append((jnp.exp(ltop - lcol) * kf).astype(bf16))
        grown.append(jnp.exp(ltop))
    inv = inverses(systems, i, j)
    us, ws = [], []
    for c in range(NCHUNK):
        low = inv[c].astype(bf16)
        inv_ref[c] = low
        both = mm(low, rights[c])
        us.append(both[:, 0:128])
        ws.append(both[:, 128:256].astype(bf16))
        w_ref[c] = ws[c]
    state = jnp.zeros((DK, HV), f32)
    for c in range(NCHUNK):
        start = state.astype(bf16)
        s_ref[c] = start
        u = (us[c] - mm(ws[c], start)).astype(bf16)
        u_ref[c] = u
        state = grown[c] * state + mm_tn(kds[c], u)
        mixed_ref[c] = (QF * (mm(qs[c], start) + mm(ps[c], u))).astype(bf16)


def backward_kernel(
    recv_ref, taps_ref, grad_ref, inv_ref, w_ref, u_ref, s_ref, q_ref, k_ref, p_ref,
    out_ref, tap_ref, ext, gext,
):
    load_tokens(recv_ref, ext)
    taps = taps_ref[...]
    betas, lrows = row_parts(recv_ref)
    lcols = lrows.T
    i, j = masks()
    strict = i > j
    gext[16 + NCHUNK * CHUNK :, :] = jnp.zeros((16, CHAN), f32)
    kept = []
    for c in range(NCHUNK):
        q, k = q_ref[c], k_ref[c]
        lcol = lcols[:, c : c + 1]
        ltop = lrows[c : c + 1, CHUNK - 1 : CHUNK]
        grow = jnp.exp(lcol)
        fade = jnp.exp(ltop - lcol)
        kd = (fade * k.astype(f32)).astype(bf16)
        grown_q = (QF * grow * q.astype(f32)).astype(bf16)
        g = grad_ref[c]
        du = QF * mm_tn(p_ref[c], g)
        ds = mm_tn(grown_q, g)
        kept.append((q, k, grow, fade, jnp.exp(ltop), kd, du, ds))
    state = jnp.zeros((DK, HV), f32)
    after, dus = [None] * NCHUNK, [None] * NCHUNK
    for c in reversed(range(NCHUNK)):
        top, kd, du, ds = kept[c][4:]
        low = state.astype(bf16)
        after[c] = low
        du = (du + mm(kd, low)).astype(bf16)
        dus[c] = du
        state = top * state + ds - mm_tn(w_ref[c], du)
    cols = []
    for c in range(NCHUNK):
        q, k, grow, fade = kept[c][:4]
        beta = betas[:, c : c + 1]
        spread = spread_of(lrows, lcols, c, i, j)
        g = grad_ref[c]
        u = u_ref[c]
        start = s_ref[c]
        pre = convolve(ext, taps, c)
        sig = sigmoid(pre)
        act = pre * sig
        v = act[:, 256:384].astype(bf16).astype(f32)
        dr = mm_tn(inv_ref[c], dus[c])
        drl = dr.astype(bf16)
        dp = (QF * spread * mm_nt(g, u)).astype(bf16)
        dt = jnp.where(strict, -spread * mm_nt(drl, u), 0.0)
        dkk = (beta * dt).astype(bf16)
        recalled = grow * mm(k, start)
        cols.append(
            jnp.sum(dt * mm_nt(k, k), -1, keepdims=True)
            + jnp.sum(dr * (v - recalled), -1, keepdims=True)
        )
        dq = mm(dp, k) + (QF * grow) * mm_nt(g, start)
        dk = (
            mm_tn(dp, q)
            + fade * mm_nt(u, after[c])
            + (mm(dkk, k) + mm_tn(dkk, k))
            - (beta * grow) * mm_nt(drl, start)
        )
        dv = beta * dr
        slope = sig * (1.0 + pre * (1.0 - sig))
        for first, part in ((0, dq), (128, dk)):
            a = act[:, first : first + 128]
            n, scale = unit(a)
            da = scale * (part - n * jnp.sum(n * part, -1, keepdims=True))
            gext[16 + c * CHUNK : 16 + (c + 1) * CHUNK, first : first + 128] = (
                da * slope[:, first : first + 128]
            )
        gext[16 + c * CHUNK : 16 + (c + 1) * CHUNK, 256:384] = dv * slope[:, 256:384]
    dbeta = jnp.concatenate(cols, 1) * betas * (1.0 - betas)
    brows = dbeta.T
    row16 = lax.broadcasted_iota(jnp.int32, (16, 128), 0)
    tap_sums = [jnp.zeros((1, CHAN), f32) for _ in range(KCONV)]
    for c in range(NCHUNK):
        here = 16 + c * CHUNK
        gpre = gext[here : here + CHUNK, :]
        total = gpre * taps[KCONV - 1 : KCONV]
        tap_sums[KCONV - 1] = tap_sums[KCONV - 1] + jnp.sum(
            gpre * ext[here : here + CHUNK, :], 0, keepdims=True
        )
        for tap in range(KCONV - 1):
            back = KCONV - 1 - tap
            total = total + gext[pl.ds(here + back, CHUNK), :] * taps[tap : tap + 1]
            tap_sums[tap] = tap_sums[tap] + jnp.sum(
                gpre * ext[pl.ds(here - back, CHUNK), :], 0, keepdims=True
            )
        out_ref[c, 0:CHUNK, :] = total.astype(bf16)
        b = brows[c : c + 1, :]
        hi = b.astype(bf16).astype(f32)
        tile = jnp.where(row16 == 0, hi, jnp.where(row16 == 1, b - hi, 0.0))
        out_ref[c, CHUNK:CHUNK_ROWS, 0:128] = tile.astype(bf16)
        out_ref[c, CHUNK:CHUNK_ROWS, 128:384] = jnp.zeros((16, 256), bf16)
    tap_ref[...] = jnp.concatenate(tap_sums + [jnp.zeros((8 - KCONV, CHAN), f32)], 0)


def head_parts(mixed_ref, gate_ref, gain, seq, head):
    a = mixed_ref[4 * seq + 2 * head].astype(f32)
    b = mixed_ref[4 * seq + 2 * head + 1].astype(f32)
    mean = (jnp.sum(a * a, -1, keepdims=True) + jnp.sum(b * b, -1, keepdims=True)) / DV
    scale = lax.rsqrt(mean + EPS)
    logit = gate_ref[seq * CHUNK : (seq + 1) * CHUNK, head * DV : (head + 1) * DV]
    n = jnp.concatenate([a, b], 1) * scale
    return n, scale, logit, sigmoid(logit), gain[:, head * DV : (head + 1) * DV]


def send_in_order(part_ref, outs):
    x = lax.axis_index("tensor")
    for d, out in enumerate(outs):
        out[...] = part_ref[pl.ds(pl.multiple_of(((x + d) % 4) * 64, 64), 64), :]


def output_kernel(
    mixed_ref, gate_ref, gain_ref, w_ref, gated_ref, o0, o1, o2, o3, part_ref
):
    gain = gain_ref[...].astype(f32)
    for seq in range(2):
        for head in range(2):
            n, _, logit, sig, own = head_parts(mixed_ref, gate_ref, gain, seq, head)
            gated_ref[seq * CHUNK : (seq + 1) * CHUNK, head * DV : (head + 1) * DV] = (
                n * own * (logit * sig)
            ).astype(bf16)
    part_ref[...] = mm_nt(gated_ref[...], w_ref[...]).astype(bf16)
    send_in_order(part_ref, (o0, o1, o2, o3))


def middle_kernel(o0, o1, o2, o3, x_ref, gain_ref, middle_ref, rows_ref):
    middle = x_ref[...] + added(o0, o1, o2, o3)
    middle_ref[...] = middle
    scale = lax.rsqrt(jnp.mean(middle * middle, -1, keepdims=True) + EPS)
    rows_ref[...] = (middle * scale * gain_ref[1:2, :]).astype(bf16)


def norm_back(g, v, gain):
    scale = lax.rsqrt(jnp.mean(v * v, -1, keepdims=True) + EPS)
    n = v * scale
    gg = g * gain
    return scale * (gg - n * jnp.mean(gg * n, -1, keepdims=True)), jnp.sum(g * n, 0, keepdims=True)


def added(o0, o1, o2, o3):
    return (o0[...].astype(f32) + o1[...].astype(f32)) + (o2[...].astype(f32) + o3[...].astype(f32))


def ffn_back_kernel(g0, g1, g2, g3, middle_ref, cot_ref, gain_ref, rows_ref, sum_ref):
    part, gain_sum = norm_back(added(g0, g1, g2, g3), middle_ref[...], gain_ref[1:2, :])
    grad = cot_ref[...].astype(f32) + part
    rows_ref[...] = grad.astype(bf16)
    sum_ref[...] = jnp.broadcast_to(gain_sum, sum_ref.shape)


def result_kernel(o0, o1, o2, o3, rows_ref):
    rows_ref[...] = added(o0, o1, o2, o3).astype(bf16)


def first_back_kernel(o0, o1, o2, o3, x_ref, grad_ref, gain_ref, out_ref):
    parts = [o[...].astype(f32) for o in (o1, o2, o3)]
    a, b, c = turned(parts, lax.axis_index("tensor"))
    part, _ = norm_back((o0[...].astype(f32) + a) + (b + c), x_ref[...], gain_ref[0:1, :])
    out_ref[...] = grad_ref[...].astype(f32) + part


def place_rows(blocks, out_ref):
    x = lax.axis_index("tensor")
    for d, block in enumerate(blocks):
        row = pl.multiple_of(((x - d + 4) % 4) * 64, 64)
        out_ref[pl.ds(row, 64), :] = block.astype(out_ref.dtype)


def place_kernel(c0, c1, c2, c3, out_ref):
    place_rows([c[...] for c in (c0, c1, c2, c3)], out_ref)


def output_back_kernel(
    c0, c1, c2, c3, mixed_ref, gate_ref, gain_ref, gated_ref, mix_ref, w_ref, gate_w_ref,
    gmix_ref, gmixed_ref, ggain_ref, part_ref, mine_hbm, other_hbm, glogit_ref, sum_ref, sem,
):
    place_rows([c[...] for c in (c0, c1, c2, c3)], gmix_ref)
    gain = gain_ref[...].astype(f32)
    grad = mm(gmix_ref[...], w_ref[...])
    sums = []
    for head in range(2):
        total = jnp.zeros((1, DV), f32)
        for seq in range(2):
            n, scale, logit, sig, own = head_parts(mixed_ref, gate_ref, gain, seq, head)
            g = grad[seq * CHUNK : (seq + 1) * CHUNK, head * DV : (head + 1) * DV]
            t = g * (logit * sig)
            total = total + jnp.sum(t * n, 0, keepdims=True)
            gn = t * own
            gm = scale * (gn - n * jnp.mean(gn * n, -1, keepdims=True))
            gmixed_ref[4 * seq + 2 * head] = gm[:, 0:128].astype(bf16)
            gmixed_ref[4 * seq + 2 * head + 1] = gm[:, 128:256].astype(bf16)
            slope = sig * (1.0 + logit * (1.0 - sig))
            glogit_ref[seq * CHUNK : (seq + 1) * CHUNK, head * DV : (head + 1) * DV] = (
                g * n * own * slope
            ).astype(bf16)
        sums.append(total)
    ggain_ref[...] = jnp.broadcast_to(jnp.concatenate(sums, 1), (8, 2 * DV))
    copies = []
    for i, (left, right) in enumerate(((gmix_ref, gated_ref), (mix_ref, glogit_ref))):
        sum_ref[i] = mm_tn(left[...], right[...]).astype(bf16).reshape(16, 2, 32, 512)
        new = split_copies(sum_ref, i, mine_hbm, other_hbm, i * 512, 512, sem)
        for copy in new:
            copy.start()
        copies += new
    part_ref[...] = mm_nt(glogit_ref[...], gate_w_ref[...])
    for copy in copies:
        copy.wait()


def ffn_kernel(
    r0, r1, r2, r3, cot_hbm, w_hbm, middle_hbm, g0, g1, g2, g3, p0, p1, p2, p3,
    hidden_hbm, ggate_hbm, gup_hbm, in_ref, cot_ref, w_ref, middle_ref, act_ref, part_ref, sem,
):
    rows = [
        pltpu.make_async_copy(ref, in_ref.at[pl.ds(d * 64, 64)], sem.at[d])
        for d, ref in enumerate((r0, r1, r2, r3))
    ]
    weights = [
        [
            pltpu.make_async_copy(
                w_hbm.at[pl.ds(r * 256, 256), pl.ds(FFN + i * FFP, FFP)],
                w_ref.at[i, pl.ds(r * 256, 256)],
                sem.at[5 + 4 * i + r],
            )
            for r in range(4)
        ]
        for i in range(3)
    ]
    cot_copy = pltpu.make_async_copy(cot_hbm, cot_ref, sem.at[4])
    middle_copy = pltpu.make_async_copy(middle_hbm, middle_ref, sem.at[17])
    for copy in rows + weights[0] + weights[1] + [cot_copy] + weights[2] + [middle_copy]:
        copy.start()
    for copy in rows + weights[0]:
        copy.wait()
    tokens = in_ref[...]
    gate = mm(tokens, w_ref[0])
    for copy in weights[1]:
        copy.wait()
    up = mm(tokens, w_ref[1])
    for copy in [cot_copy] + weights[2]:
        copy.wait()
    ghidden = mm(cot_ref[...], w_ref[2])
    sig = sigmoid(gate)
    silu = gate * sig
    ggate = (ghidden * up * (sig * (1.0 + gate * (1.0 - sig)))).astype(bf16)
    gup = (ghidden * silu).astype(bf16)
    hidden = (silu * up).astype(bf16)
    outs = []

    def send(source, target):
        outs.append(pltpu.make_async_copy(source, target, sem.at[18 + len(outs)]))
        outs[-1].start()

    for place, (value, target) in enumerate(
        ((ggate, ggate_hbm), (gup, gup_hbm), (hidden, hidden_hbm))
    ):
        act_ref[place] = value
        send(act_ref.at[place], target)
    part_ref[0] = (mm_nt(ggate, w_ref[0]) + mm_nt(gup, w_ref[1])).astype(bf16)
    for d, target in enumerate((g0, g1, g2, g3)):
        send(part_ref.at[0, pl.ds(d * 64, 64)], target)
    part = mm_nt(hidden, w_ref[2])
    middle_copy.wait()
    part_ref[1, 0:64, :] = (part[0:64] + middle_ref[...]).astype(bf16)
    part_ref[1, 64:256, :] = part[64:256].astype(bf16)
    for d, target in enumerate((p0, p1, p2, p3)):
        send(part_ref.at[1, pl.ds(d * 64, 64)], target)
    for copy in outs:
        copy.wait()


def split_copies(sum_ref, index, mine_hbm, other_hbm, first, width, sem):
    core = lax.axis_index("seq") % 2
    return [
        pltpu.make_async_copy(
            sum_ref.at[index, :, core if k == 0 else 1 - core],
            out.at[:, :, pl.ds(first, width)],
            sem.at[2 * index + k],
        )
        for k, out in enumerate((mine_hbm, other_hbm))
    ]


def ffn_weight_kernel(
    r0, r1, r2, r3, cot_ref, hidden_ref, ggate_ref, gup_ref, mine_hbm, other_hbm, in_ref, sum_ref, sem
):
    for d, ref in enumerate((r0, r1, r2, r3)):
        in_ref[d * 64 : (d + 1) * 64, :] = ref[...]
    copies = []
    for i, (left, right) in enumerate(
        ((in_ref, ggate_ref), (in_ref, gup_ref), (cot_ref, hidden_ref))
    ):
        sum_ref[i] = mm_tn(left[...], right[...]).astype(bf16).reshape(16, 2, 32, FFP)
        new = split_copies(sum_ref, i, mine_hbm, other_hbm, i * FFP, FFP, sem)
        for copy in new:
            copy.start()
        copies += new
    for copy in copies:
        copy.wait()


def second_sum_kernel(mine_e, got_e, mine_f, got_f, out_ref):
    out_ref[:, :, 0:FFN] = (mine_e[...].astype(f32) + got_e[...].astype(f32)).astype(bf16)
    out_ref[:, :, FFN:] = (mine_f[...].astype(f32) + got_f[...].astype(f32)).astype(bf16)


def second_split_kernel(in_ref, out_ref, gate_ref, a_ref, b_ref, c_ref):
    out_ref[...] = in_ref[:, 0:512].astype(f32)
    gate_ref[...] = in_ref[:, 512:1024].astype(f32)
    for i, ref in enumerate((a_ref, b_ref, c_ref)):
        ref[...] = in_ref[:, FFN + i * FFP : FFN + i * FFP + FF].astype(f32)


def core_split(value, core, mine_ref, other_ref, y):
    value = value.reshape(4, 2, 32, value.shape[-1])
    first, second = value[:, 0], value[:, 1]
    mine = jnp.where(core == 0, first, second)
    other = jnp.where(core == 0, second, first)
    rows = slice(y * 128, (y + 1) * 128)
    mine_ref[rows, :] = mine.reshape(128, W1_COLS)
    other_ref[rows, :] = other.reshape(128, W1_COLS)


def coded(small):
    hi = small.astype(bf16).astype(f32)
    lo = (small - hi).astype(bf16).astype(f32)
    tile = jnp.concatenate([hi, lo], 0)
    tile = jnp.concatenate([tile, jnp.zeros((16, W1_COLS - 1024), f32)], 1)
    return tile.astype(bf16), hi + lo


def decoded(tile):
    tile = tile[:, 0:1024].astype(f32)
    return tile[0:8] + tile[8:16]


def project_back_kernel(
    recv_ref,
    mix_ref,
    gate_part_ref,
    w_ref,
    x_ref,
    taps_ref,
    ggain_ref,
    fgain_ref,
    part_ref,
    mine_ref,
    other_ref,
    small_ref,
    dproj_ref,
    row_ref,
):
    s = lax.axis_index("seq")
    core, head_here = s % 2, (s // 2) % 2
    row = lax.broadcasted_iota(jnp.int32, (128, 128), 0)
    for seq in range(2):
        rows = slice(seq * CHUNK, (seq + 1) * CHUNK)
        beta = jnp.zeros((128, 128), f32)
        for head in range(2):
            ja = 4 * seq + 2 * head
            a, b = recv_ref.at[ja], recv_ref.at[ja + 1]
            for first in (0, 128):
                total = a[0:CHUNK, first : first + 128].astype(f32) + b[
                    0:CHUNK, first : first + 128
                ].astype(f32)
                place = 2 * first + head * 128
                dproj_ref[rows, place : place + 128] = total.astype(bf16)
            dproj_ref[rows, 512 + head * 256 : 640 + head * 256] = a[0:CHUNK, 256:384]
            dproj_ref[rows, 640 + head * 256 : 768 + head * 256] = b[0:CHUNK, 256:384]
            both = a[CHUNK:CHUNK_ROWS, 0:128].astype(f32) + b[CHUNK:CHUNK_ROWS, 0:128].astype(f32)
            beta = jnp.where(row == head, both[0:1] + both[1:2], beta)
        dproj_ref[rows, BETA:W1_COLS] = beta.T.astype(bf16)
    part = mm_nt(dproj_ref[...], w_ref[...]) + gate_part_ref[...]
    part_ref[...] = part.astype(bf16)
    xs = x_ref[...]
    mix_sum = jnp.sum(
        part * (xs * lax.rsqrt(jnp.mean(xs * xs, -1, keepdims=True) + EPS)), 0, keepdims=True
    )
    row_ref[...] = jnp.zeros((8, 1024), f32)
    for first, base in (
        (0, head_here * 128),
        (128, 256 + head_here * 128),
        (256, 512 + head_here * 256 + core * 128),
    ):
        lanes = pl.ds(pl.multiple_of(base, 128), 128)
        row_ref[0:8, lanes] = taps_ref[0:8, first : first + 128]
    row_ref[4:5, 0:512] = ggain_ref[0:1, :]
    row_ref[5:6, :] = mix_sum
    row_ref[6:7, :] = fgain_ref[0:1, :]
    tile, value = coded(row_ref[...])
    small_ref[...] = value
    other_ref[512:528, :] = tile
    for y in range(4):
        value = mm_tn(mix_ref[:, y * 256 : (y + 1) * 256], dproj_ref[...]).astype(bf16)
        core_split(value, core, mine_ref, other_ref, y)


def turned(got, index):
    even = index % 2 == 0
    return jnp.where(even, got[2], got[0]), got[1], jnp.where(even, got[0], got[2])


def fold_kernel(axis, base_ref, *refs):
    count = 1 if axis == "batch" else 3
    got, small_ref, outs, small_out = refs[:count], refs[count], refs[count + 1 : -1], refs[-1]
    y, z = lax.axis_index("batch"), lax.axis_index("seq") // 2
    here = y if axis == "batch" else z
    size = outs[0].shape[0]
    parts = [decoded(g[4 * size : 4 * size + 16, :]) for g in got]
    if count == 1:
        small = small_ref[...] + parts[0]
    else:
        a, b, c = turned(parts, y)
        small = (small_ref[...] + a) + (b + c)
    tile, value = coded(small)
    small_out[...] = value
    for d, out in enumerate(outs):
        rows = pl.ds(pl.multiple_of(((here + d) % 4) * size, 32), size)
        total = base_ref[rows, :].astype(f32)
        for g in got:
            total = total + g[rows, :].astype(f32)
        out[0:size, :] = total.astype(out.dtype)
        if d > 0:
            out[size : size + 16, :] = tile


def first_out_kernel(
    base_ref, g1, g2, g3, small_ref,
    q_ref, k_ref, v_ref, beta_ref, tap_q_ref, tap_k_ref, tap_v_ref, out_gain_ref, gain_ref,
):
    got = (g1, g2, g3)
    total = base_ref[...]
    for g in got:
        total = total + g[0:32, :].astype(f32)
    q_ref[...] = total[:, 0:256]
    k_ref[...] = total[:, 256:512]
    v_ref[...] = total[:, 512:1024]
    beta_ref[...] = total[:, BETA:W1_COLS].T[0:2, :]
    a, b, c = turned([decoded(g[32:48, :]) for g in got], lax.axis_index("seq") // 2)
    small = (small_ref[...] + a) + (b + c)
    tap_q_ref[...] = small[0:4, 0:256]
    tap_k_ref[...] = small[0:4, 256:512]
    tap_v_ref[...] = small[0:4, 512:1024]
    out_gain_ref[...] = small[4:5, 0:512]
    place = (lax.axis_index("batch") * 8 + lax.axis_index("seq")) * 32
    gain_ref[...] = pltpu.roll(small, (1024 - place) % 1024, 1)[:, 0:128]


def gain_kernel(g0, g1, g2, g3, mix_ref, ffn_ref):
    a, b, c = turned([g1[...], g2[...], g3[...]], lax.axis_index("tensor"))
    total = (g0[...] + a) + (b + c)
    mix_ref[...] = total[5:6, 0:32]
    ffn_ref[...] = total[6:7, 0:32]


vmem = pl.BlockSpec(memory_space=pltpu.VMEM)
hbm = pl.BlockSpec(memory_space=pl.ANY)


def call(kernel, outs, *args, scratch=(), in_specs=None, out_specs=None, windowed=False, name=None, mb=8):
    grid = {"grid": (1,)} if windowed else {}
    return pl.pallas_call(
        kernel,
        **grid,
        out_shape=[jax.ShapeDtypeStruct(shape, dtype) for shape, dtype in outs],
        in_specs=in_specs or [vmem] * len(args),
        out_specs=out_specs or [vmem] * len(outs),
        scratch_shapes=list(scratch),
        compiler_params=pltpu.CompilerParams(vmem_limit_bytes=mb * 1024 * 1024),
        cost_estimate=pl.CostEstimate(flops=COST, bytes_accessed=COST, transcendentals=0),
        name=name,
    )(*args)


def fold(axis, base, got, small, size, name):
    outs = [((size, W1_COLS), f32)] + [((size + 16, W1_COLS), bf16)] * 3 + [((8, 1024), f32)]
    *out, small = call(partial(fold_kernel, axis), outs, base, *got, small, name=name, mb=12)
    return out, small


def per_device(
    inputs,
    decay_rate,
    cotangent,
    mix_gain,
    query_weight,
    key_weight,
    value_weight,
    gate_weight,
    beta_weight,
    conv_query,
    conv_key,
    conv_value,
    out_gain,
    output_weight,
    ffn_gain,
    ffn_gate,
    ffn_up,
    ffn_down,
):
    s = lax.axis_index("seq")
    x = lax.axis_index("tensor")
    head, half = (s // 2) % 2, s % 2
    tokens = inputs.reshape(256, 1024)
    cot = cotangent.reshape(256, 1024)

    logs = jnp.cumsum(jnp.log(decay_rate), 1).transpose(0, 2, 1).reshape(4, CHUNK)
    logs = jnp.pad(logs, ((0, 4), (0, 0)))
    (shard1,) = call(
        first_pack_kernel,
        [((32, W1_COLS), bf16)],
        query_weight,
        key_weight,
        value_weight,
        beta_weight.T,
        mix_gain[None],
        ffn_gain[None],
        name="first_pack",
        mb=56,
    )
    column = jnp.stack([shard1] + [move_z(shard1, d) for d in (1, 2, 3)])

    output_weight, column, logs = lax.optimization_barrier((output_weight, column, logs))
    (shard2,) = call(
        second_pack_kernel,
        [((32, W2_COLS), bf16)],
        output_weight,
        gate_weight,
        ffn_gate,
        ffn_up,
        ffn_down,
        name="second_pack",
        mb=56,
    )
    own = [column] + [move_y(column, d) for d in (1, 2, 3)]
    sib = [move_core(v) for v in own]
    w2 = lax.all_gather(shard2, ("batch", "seq"), axis=0, tiled=True)

    taps = jnp.concatenate(
        [
            lax.dynamic_slice_in_dim(conv_query.T, head * DK, DK, 1),
            lax.dynamic_slice_in_dim(conv_key.T, head * DK, DK, 1),
            lax.dynamic_slice_in_dim(conv_value.T, head * DV + half * HV, HV, 1),
        ],
        1,
    ).astype(f32)
    taps = jnp.pad(taps, ((0, 8 - KCONV), (0, 0)))
    gain_row = out_gain[None]
    own_tokens = pick(tokens.reshape(4, 64, 1024), x)
    cot4 = cot.reshape(4, 64, 1024)
    own_cot = pick(cot4, x)
    cot_turned = jnp.concatenate([pick(cot4, (x - d) % 4) for d in range(4)], 0)

    w1, mix_input, send, gains = call(
        project_kernel,
        [
            ((1024, W1_COLS), bf16),
            ((256, 1024), bf16),
            ((8, CHUNK_ROWS, CHAN), bf16),
            ((8, 1024), f32),
        ],
        *own,
        *sib,
        tokens,
        logs,
        scratch=[
            pltpu.SemaphoreType.DMA((38,)),
            pltpu.VMEM((1024, W1_COLS), bf16),
            pltpu.VMEM((256, 1024), f32),
            pltpu.VMEM((8, CHUNK), f32),
        ],
        in_specs=[hbm] * 10,
        out_specs=[hbm] + [vmem] * 3,
        name="project",
        mb=56,
    )
    recv = lax.all_to_all(send, "seq", 0, 0)
    square = ((NCHUNK, 128, 128), bf16)
    mixed, *saved = call(
        forward_kernel,
        [square] * 8,
        recv,
        taps,
        scratch=[pltpu.VMEM((16 + NCHUNK * CHUNK, CHAN), f32)],
        name="delta_forward",
        mb=56,
    )
    mixed = lax.all_to_all(mixed, "seq", 0, 0)
    out_w = pl.BlockSpec((1024, 512), lambda i: (0, 0))
    gate_w = pl.BlockSpec((1024, 512), lambda i: (0, 1))
    (gate_logit,) = call(
        gate_kernel,
        [((256, 512), f32)],
        mix_input,
        w2,
        in_specs=[vmem, gate_w],
        windowed=True,
        name="gate",
        mb=56,
    )
    quarter = ((64, 1024), bf16)
    gated, *pieces = call(
        output_kernel,
        [((256, 512), bf16)] + [quarter] * 4,
        mixed,
        gate_logit,
        gain_row,
        w2,
        in_specs=[vmem] * 3 + [out_w],
        scratch=[pltpu.VMEM((256, 1024), bf16)],
        windowed=True,
        name="output",
        mb=56,
    )
    middle, ffn_rows = call(
        middle_kernel,
        [((64, 1024), f32), quarter],
        pieces[0],
        *[move_x(pieces[d], d) for d in (1, 2, 3)],
        own_tokens,
        gains,
        name="middle",
        mb=56,
    )
    ffn_blocks = gather_x(ffn_rows)
    hidden_shape = ((256, FFP), bf16)
    ffn_out = call(
        ffn_kernel,
        [quarter] * 8 + [hidden_shape] * 3,
        *ffn_blocks,
        cot_turned,
        w2,
        middle,
        in_specs=[hbm] * 7,
        out_specs=[hbm] * 11,
        scratch=[
            pltpu.VMEM((256, 1024), bf16),
            pltpu.VMEM((256, 1024), bf16),
            pltpu.VMEM((3, 1024, FFP), bf16),
            pltpu.VMEM((64, 1024), f32),
            pltpu.VMEM((3, 256, FFP), bf16),
            pltpu.VMEM((2, 256, 1024), bf16),
            pltpu.SemaphoreType.DMA((29,)),
        ],
        name="ffn",
        mb=56,
    )
    gpieces, rpieces, (hidden, ggate, gup) = ffn_out[:4], tuple(ffn_out[4:8]), ffn_out[8:]
    got = [move_x(gpieces[d], -d) for d in (1, 2, 3)]
    mine_f, other_f = call(
        ffn_weight_kernel,
        [((16, 32, 3 * FFP), bf16)] * 2,
        *ffn_blocks,
        cot_turned,
        hidden,
        ggate,
        gup,
        out_specs=[hbm, hbm],
        scratch=[
            pltpu.VMEM((256, 1024), bf16),
            pltpu.VMEM((3, 16, 2, 32, FFP), bf16),
            pltpu.SemaphoreType.DMA((6,)),
        ],
        name="ffn_weight",
        mb=56,
    )
    middle, other_f = lax.optimization_barrier((middle, other_f))
    grad_rows, ffn_gain_sum = call(
        ffn_back_kernel,
        [quarter, ((8, 1024), f32)],
        gpieces[0],
        *got,
        middle,
        own_cot,
        gains,
        name="ffn_back",
        mb=56,
    )
    other_f, grad_rows = lax.optimization_barrier((other_f, grad_rows))
    got_f = move_core(other_f)
    mix_blocks = gather_x(grad_rows)
    grad_mix, gmixed, ggain, gate_part, mine_e, other_e = call(
        output_back_kernel,
        [
            ((256, 1024), bf16),
            ((8, CHUNK, 128), bf16),
            ((8, 512), f32),
            ((256, 1024), f32),
            ((16, 32, FFN), bf16),
            ((16, 32, FFN), bf16),
        ],
        *mix_blocks,
        mixed,
        gate_logit,
        gain_row,
        gated,
        mix_input,
        w2,
        w2,
        in_specs=[vmem] * 9 + [out_w, gate_w],
        out_specs=[vmem] * 4 + [hbm] * 2,
        scratch=[
            pltpu.VMEM((256, 512), bf16),
            pltpu.VMEM((2, 16, 2, 32, 512), bf16),
            pltpu.SemaphoreType.DMA((4,)),
        ],
        windowed=True,
        name="output_back",
        mb=56,
    )
    rpieces, gmixed = lax.optimization_barrier((rpieces, gmixed))
    rgot = tuple(move_x(rpieces[d], -d) for d in (1, 2, 3))
    gmixed = lax.all_to_all(gmixed, "seq", 0, 0)
    grad_w2 = pl.pallas_call(
        second_sum_kernel,
        grid=(4,),
        out_shape=jax.ShapeDtypeStruct((16, 32, W2_COLS), bf16),
        in_specs=[
            pl.BlockSpec((4, 32, cols), lambda i: (i, 0, 0)) for cols in (FFN, FFN, 3 * FFP, 3 * FFP)
        ],
        out_specs=pl.BlockSpec((4, 32, W2_COLS), lambda i: (i, 0, 0)),
        compiler_params=pltpu.CompilerParams(vmem_limit_bytes=56 * 1024 * 1024),
        cost_estimate=pl.CostEstimate(flops=COST, bytes_accessed=COST, transcendentals=0),
        name="second_sum",
    )(mine_e, move_core(other_e), mine_f, got_f)
    gmixed, grad_w2 = lax.optimization_barrier((gmixed, grad_w2))
    same_core = [[y * 8 + z * 2 + c for y in range(4) for z in range(4)] for c in range(2)]
    grad_w2 = lax.psum_scatter(
        grad_w2.reshape(512, W2_COLS),
        ("batch", "seq"),
        scatter_dimension=0,
        axis_index_groups=same_core,
        tiled=True,
    )
    gsend, gtaps = call(
        backward_kernel,
        [((8, CHUNK_ROWS, CHAN), bf16), ((8, CHAN), f32)],
        recv,
        taps,
        gmixed,
        *saved,
        scratch=[
            pltpu.VMEM((16 + NCHUNK * CHUNK, CHAN), f32),
            pltpu.VMEM((32 + NCHUNK * CHUNK, CHAN), f32),
        ],
        name="delta_backward",
        mb=56,
    )
    gsend, rgot = lax.optimization_barrier((gsend, rgot))
    grecv = lax.all_to_all(gsend, "seq", 0, 0)
    (result_rows,) = call(
        result_kernel,
        [quarter],
        rpieces[0],
        *rgot,
        name="result_rows",
        mb=56,
    )
    result_blocks = gather_x(result_rows)
    grecv, result_blocks = lax.optimization_barrier((grecv, result_blocks))
    part, mine, other, small = call(
        project_back_kernel,
        [
            ((256, 1024), bf16),
            ((512, W1_COLS), bf16),
            ((528, W1_COLS), bf16),
            ((8, 1024), f32),
        ],
        grecv,
        mix_input,
        gate_part,
        w1,
        tokens,
        gtaps,
        ggain,
        ffn_gain_sum,
        scratch=[
            pltpu.VMEM((256, W1_COLS), bf16),
            pltpu.VMEM((8, 1024), f32),
        ],
        name="project_back",
        mb=28,
    )
    out, small = fold("batch", mine, [move_core(other)], small, 128, "first_core")
    got = [move_y(out[d], d) for d in (1, 2, 3)]
    part_2 = move_x(part, 2)
    (result,) = call(place_kernel, [((256, 1024), f32)], *result_blocks, name="result")
    got, result = lax.optimization_barrier((got, result))
    out, small = fold("seq", out[0], got, small, 32, "first_y")
    out, part = lax.optimization_barrier((out, part))
    got = [move_z(out[d], d) for d in (1, 2, 3)]
    (grad_inputs,) = call(
        first_back_kernel,
        [((256, 1024), f32)],
        part,
        move_x(part, 1),
        part_2,
        move_x(part, 3),
        tokens,
        grad_mix,
        gains,
        name="first_back",
        mb=14,
    )
    grad_q, grad_k, grad_v, grad_beta, tap_q, tap_k, tap_v, grad_out_gain, gain_rows = call(
        first_out_kernel,
        [
            ((32, 256), f32),
            ((32, 256), f32),
            ((32, 512), f32),
            ((2, 32), f32),
            ((4, 256), f32),
            ((4, 256), f32),
            ((4, 512), f32),
            ((1, 512), f32),
            ((8, 128), f32),
        ],
        out[0],
        *got,
        small,
        name="first_z",
    )
    grad_out_w, grad_gate_w, grad_fgate, grad_fup, grad_fdown = call(
        second_split_kernel,
        [((32, 512), f32)] * 2 + [((32, FF), f32)] * 3,
        grad_w2,
        name="second_split",
        mb=10,
    )
    grad_mix_gain, grad_ffn_gain = call(
        gain_kernel, [((1, 32), f32)] * 2, *gather_x(gain_rows), name="gain_sums"
    )
    return (
        result.reshape(2, 128, 1024),
        grad_inputs.reshape(2, 128, 1024),
        grad_mix_gain[0],
        grad_q,
        grad_k,
        grad_v,
        grad_gate_w,
        grad_beta.T,
        tap_q.T,
        tap_k.T,
        tap_v.T,
        grad_out_gain[0],
        grad_out_w,
        grad_ffn_gain[0],
        grad_fgate,
        grad_fup,
        grad_fdown,
    )


def solution(mesh):
    rows = ("batch", "seq")
    split = P(rows, "tensor")
    tokens = P("batch", "seq", None)
    taps = P("tensor", None)
    placed = (
        tokens,
        P("batch", "seq", "tensor"),
        tokens,
        P(rows),
        split,
        split,
        split,
        split,
        split,
        taps,
        taps,
        taps,
        P("tensor"),
        split,
        P(rows),
        split,
        split,
        split,
    )
    return jax.shard_map(
        per_device,
        mesh=mesh,
        in_specs=placed,
        out_specs=(
            tokens,
            tokens,
            P(rows),
            split,
            split,
            split,
            split,
            split,
            taps,
            taps,
            taps,
            P("tensor"),
            split,
            P(rows),
            split,
            split,
            split,
        ),
        check_vma=False,
    )
```
